32 devices in a mesh: site: 4 (over z), bond: 8 (over y, x, core).
Axes of the slice: x: 2, y: 2, z: 4, core: 2. Of those that a mesh axis runs over, the one named last changes fastest.
Arguments:
- left_env: float32 [4, 512, 16, 512], P('site', 'bond'), may hold values from -6 to 6
- right_env: float32 [4, 512, 16, 512], P('site', 'bond'), may hold values from -6 to 6
- left_site: float32 [4, 512, 4, 512], P('site'), may hold values from -0.125 to 0.125
- right_site: float32 [4, 512, 4, 512], P('site'), may hold values from -0.125 to 0.125
- left_mpo: float32 [4, 16, 16, 4, 4], P('site'), may hold values from -1.5 to 1.5
- right_mpo: float32 [4, 16, 16, 4, 4], P('site'), may hold values from -1.5 to 1.5
Outputs:
- new_left: float32 [4, 512, 16, 512], P('site', 'bond')
- new_right: float32 [4, 512, 16, 512], P('site', 'bond')
The draws below stay inside these ranges and needn't reach their ends.
All inputs are finite; a program needn't handle non-finite values.
Results may differ from the reference program's by a relative error of at most 0.0001.
Values sent between devices are 32-bit elements; how exact they have to be, the bound alone decides.
No kernel may reach another device: no remote copies, remote signals or barrier semaphores. Data moves between devices by JAX's collectives and lax.ppermute only.
A program may use at most 128 MiB of HBM per device.

```python
import jax
import jax.numpy as jnp
from jax import lax

D = 512
W = 16
PHYS = 4
SEGS = 4


def levels(stream_key, dims, split, low, top_value):
    factor_of = 1.0
    for axis_at, shards_of in split:
        heights = jax.random.uniform(jax.random.fold_in(jax.random.fold_in(stream_key, 6), axis_at), (shards_of,), jnp.float32, low / len(split), top_value / len(split))
        factor_of = factor_of * jnp.repeat(jnp.exp(heights), dims[axis_at] // shards_of).reshape((-1,) + (1,) * (len(dims) - 1 - axis_at))
    return factor_of


def bell_draw(key, extent, scale, reach, cuts=(), kind=jnp.bfloat16):
    factor_of = levels(key, extent, cuts, -0.22, 0.18) if cuts else 1.0
    array = jax.random.normal(key, extent, jnp.float32) * scale * factor_of
    return jnp.minimum(jnp.maximum(array, -reach), reach).astype(kind)


def setup_inputs(seed: int = 0) -> dict:
    seeds = jax.random.split(jax.random.key(seed), 7)
    left_env = bell_draw(seeds[0], (SEGS, D, W, D), 1.0, 6.0, ((0, 4), (1, 8)), jnp.float32)
    right_env = bell_draw(seeds[1], (SEGS, D, W, D), 1.0, 6.0, ((0, 4), (1, 8)), jnp.float32)
    left_site = bell_draw(seeds[2], (SEGS, D, PHYS, D), (D * PHYS) ** -0.5, 0.125, ((0, 4),), jnp.float32)
    right_site = bell_draw(seeds[3], (SEGS, D, PHYS, D), (D * PHYS) ** -0.5, 0.125, ((0, 4),), jnp.float32)
    left_mpo = bell_draw(seeds[4], (SEGS, W, W, PHYS, PHYS), W ** -0.5, 1.5, ((0, 4),), jnp.float32)
    right_mpo = bell_draw(seeds[5], (SEGS, W, W, PHYS, PHYS), W ** -0.5, 1.5, ((0, 4),), jnp.float32)
    return dict(left_env=left_env, right_env=right_env, left_site=left_site, right_site=right_site, left_mpo=left_mpo, right_mpo=right_mpo)


def grow_env(environ, tensor, operator):
    first_part = jnp.einsum("awc,asb->wcsb", environ, tensor, precision=lax.Precision.HIGHEST)
    second_part = jnp.einsum("wcsb,wvst->bvct", first_part, operator, precision=lax.Precision.HIGHEST)
    result = jnp.dot(second_part.reshape(D * W, D * PHYS), tensor.reshape(D * PHYS, D), precision=lax.Precision.HIGHEST)
    return result.reshape(D, W, D)


def reference(left_env, right_env, left_site, right_site, left_mpo, right_mpo):
    grown_left = []
    grown_right = []
    for segment in range(SEGS):
        grown_left.append(grow_env(left_env[segment], left_site[segment], left_mpo[segment]))
        grown_right.append(grow_env(right_env[segment], right_site[segment], jnp.transpose(right_mpo[segment], (1, 0, 2, 3))))
    new_left = jnp.stack([left_env[0]] + grown_left[:-1])
    new_right = jnp.stack(grown_right[1:] + [right_env[SEGS - 1]])
    return new_left, new_right
```

```python
import functools

import jax
import jax.numpy as jnp
from jax import lax
from jax.experimental import pallas as pl
from jax.experimental.pallas import tpu as pltpu
from jax.sharding import PartitionSpec as P

F32 = jnp.float32
BF16 = jnp.bfloat16
VMEM_BYTES = 48 << 20


def factors(n):
    pair = 2 if n % 2 == 0 else 1
    rest = n // pair
    inner = max(d for d in range(1, rest + 1) if rest % d == 0 and d * d <= rest)
    return rest // inner, inner, pair


def shares(total, weights, unit):
    cuts, done, seen = [], 0, 0
    for weight in weights:
        seen += weight
        upto = (total * seen // sum(weights)) // unit * unit
        cuts.append(upto - done)
        done = upto
    cuts[-1] += total - done
    return [c for c in cuts if c]


def parts(x):
    high = x.astype(BF16)
    return high, (x - high.astype(F32)).astype(BF16)


def parts_outside(x):
    high = lax.reduce_precision(x, 8, 7)
    return high.astype(BF16), (x - high).astype(BF16)


def dot(a, b):
    return jnp.dot(a, b, preferred_element_type=F32)


def dot_parts(ah, al, bh, bl):
    return dot(ah, bh) + (dot(ah, bl) + dot(al, bh))


def call(body, name, grid, ins, outs, flops, *operands):
    specs = [spec for spec, _ in outs]
    shapes = [shape for _, shape in outs]
    size = lambda x: x.size * x.dtype.itemsize
    return pl.pallas_call(
        body,
        name=name,
        grid=grid,
        in_specs=ins,
        out_specs=specs,
        out_shape=shapes,
        compiler_params=pltpu.CompilerParams(vmem_limit_bytes=VMEM_BYTES),
        cost_estimate=pl.CostEstimate(
            flops=flops,
            bytes_accessed=sum(map(size, operands)) + sum(map(size, shapes)),
            transcendentals=0,
        ),
    )(*operands)


def whole(x):
    zeros = (0,) * x.ndim
    return pl.BlockSpec(x.shape, lambda *_: zeros)


def rows_kernel(n, *refs):
    envs, (sh, sl, mh, ml, uh, ul) = refs[:n], refs[n:]
    states = sh.shape[0]
    width = envs[0].shape[1]
    group = mh.shape[0] // (states * width)
    done = 0
    for env in envs:
        rows = env.shape[0]
        eh, el = parts(env[...].reshape(rows * width, env.shape[2]))
        first = [parts(dot_parts(eh, el, sh[t], sl[t])) for t in range(states)]
        for g in range(rows // group):
            at = slice(g * group * width, (g + 1) * group * width)
            kh = jnp.concatenate([h[at] for h, _ in first], 0)
            kl = jnp.concatenate([l[at] for _, l in first], 0)
            second = dot_parts(mh[...], ml[...], kh, kl)
            h, l = parts(second)
            to = slice(done, done + group * states)
            uh[:, to, :] = h.reshape(width, group * states, h.shape[1])
            ul[:, to, :] = l.reshape(width, group * states, l.shape[1])
            done += group * states


def rows_part(envs, block, tensor, operator):
    rows, width, depth = envs[0].shape
    states, _, columns = tensor[0].shape
    made = len(envs) * block * states
    out = jax.ShapeDtypeStruct((width, len(envs) * rows * states, columns), BF16)
    out_spec = pl.BlockSpec((width, made, columns), lambda i: (0, i, 0))
    count = len(envs) * rows
    return call(
        functools.partial(rows_kernel, len(envs)),
        "rows_part",
        (rows // block,),
        [pl.BlockSpec((block, width, depth), lambda i: (i, 0, 0))] * len(envs)
        + [whole(x) for x in (*tensor, *operator)],
        [(out_spec, out)] * 2,
        6 * count * width * states * columns * (depth + operator[0].shape[0]),
        *envs,
        *tensor,
        *operator,
    )


def close_left_kernel(n, sent, sh, sl, *refs):
    uhs, uls, (away, kept) = refs[:n], refs[n : 2 * n], refs[2 * n :]
    for v in range(kept.shape[0]):
        h = jnp.concatenate([u[v] for u in uhs], 0)
        l = jnp.concatenate([u[v] for u in uls], 0)
        out = dot_parts(sh[...], sl[...], h, l)
        away[v] = out[:sent]
        kept[v] = out[sent:]


def close_left(pieces, ket, start, count, sent):
    columns = pieces[0][0].shape[2]
    made = ket[0].shape[0]
    uhs = [h for h, _ in pieces]
    uls = [l for _, l in pieces]
    block = min(count, 4)
    u_spec = lambda u: pl.BlockSpec((block, u.shape[1], columns), lambda i: (i + start // block, 0, 0))
    outs = [
        (
            pl.BlockSpec((block, m, columns), lambda i: (i, 0, 0)),
            jax.ShapeDtypeStruct((count, m, columns), F32),
        )
        for m in (sent, made - sent)
    ]
    return call(
        functools.partial(close_left_kernel, len(pieces), sent),
        "close_left",
        (count // block,),
        [whole(x) for x in ket] + [u_spec(u) for u in (*uhs, *uls)],
        outs,
        6 * made * ket[0].shape[1] * columns * count,
        *ket,
        *uhs,
        *uls,
    )


def slices_kernel(n, *refs):
    envs, (sh, sl, xh, xl) = refs[:n], refs[n:]
    for w in range(envs[0].shape[0]):
        eh, el = parts(jnp.concatenate([env[w] for env in envs], 0))
        h, l = parts(dot_parts(sh[...], sl[...], eh, el))
        xh[w] = h
        xl[w] = l


def slices_part(envs, ket):
    width, rows, depth = envs[0].shape
    made = ket[0].shape[0]
    out = jax.ShapeDtypeStruct((width, made, depth), BF16)
    spec = lambda r: pl.BlockSpec((1, r, depth), lambda i: (i, 0, 0))
    return call(
        functools.partial(slices_kernel, len(envs)),
        "slices_part",
        (width,),
        [spec(rows)] * len(envs) + [whole(x) for x in ket],
        [(spec(made), out)] * 2,
        6 * made * len(envs) * rows * width * depth,
        *envs,
        *ket,
    )


def close_right_kernel(n, *refs):
    xhs, xls, (mh, ml, sh, sl, out) = refs[:n], refs[n : 2 * n], refs[2 * n :]
    states, depth, columns = sh.shape
    rows, width = out.shape[0], out.shape[1]
    group = mh.shape[0] // (states * width)
    highs, lows = [], []
    for g in range(rows // group):
        at = slice(g * group * states, (g + 1) * group * states)
        kh = jnp.concatenate([x[w, at, :] for x in xhs for w in range(x.shape[0])], 0)
        kl = jnp.concatenate([x[w, at, :] for x in xls for w in range(x.shape[0])], 0)
        h, l = parts(dot_parts(mh[...], ml[...], kh, kl))
        highs.append(h)
        lows.append(l)
    span = group * width
    pick = lambda t, ys: jnp.concatenate([y[t * span : (t + 1) * span] for y in ys], 0)
    yh = jnp.concatenate([pick(t, highs) for t in range(states)], 1)
    yl = jnp.concatenate([pick(t, lows) for t in range(states)], 1)
    flat = lambda s: s[...].reshape(states * depth, columns)
    total = dot_parts(yh, yl, flat(sh), flat(sl))
    out[...] = total.reshape(rows, width, columns)


def close_right(pieces, operator, tensor, start, count, width):
    states, depth, columns = tensor[0].shape
    xhs = [h for h, _ in pieces]
    xls = [l for _, l in pieces]
    spec = lambda x: pl.BlockSpec((x.shape[0], count * states, depth), lambda i: (0, start // count, 0))
    (out,) = call(
        functools.partial(close_right_kernel, len(pieces)),
        "close_right",
        (1,),
        [spec(x) for x in (*xhs, *xls)] + [whole(x) for x in (*operator, *tensor)],
        [
            (
                pl.BlockSpec((count, width, columns), lambda i: (0, 0, 0)),
                jax.ShapeDtypeStruct((count, width, columns), F32),
            )
        ],
        6 * count * width * states * depth * (columns + operator[0].shape[0]),
        *xhs,
        *xls,
        *operator,
        *tensor,
    )
    return out


def local(sizes, left_env, right_env, left_site, right_site, left_mpo, right_mpo):
    outer, inner, pair = sizes
    n = outer * inner * pair
    position = lax.axis_index("bond")
    at_outer = position // (inner * pair)
    at_inner = position // pair % inner
    at_pair = position % pair
    index = lambda o, i, p: (o % outer * inner + i % inner) * pair + p % pair

    def moved(x, o=0, i=0, p=0):
        route = []
        for d in range(n):
            do, di, dp = d // (inner * pair), d // pair % inner, d % pair
            route.append((d, index(do + o, di + i, dp + p)))
        return lax.ppermute(x, "bond", route)

    def handed(x, distance, p=0):
        chain = lax.axis_size("site")
        route = []
        for k in range(chain):
            if 0 <= k + distance < chain:
                for d in range(n):
                    to = d - d % pair + (d + p) % pair
                    route.append((k * n + d, (k + distance) * n + to))
        return lax.ppermute(x, ("site", "bond"), route)

    left_e, right_e = left_env[0], right_env[0]
    left_t, right_t = left_site[0], right_site[0]
    rows, width, depth = left_e.shape
    states = left_t.shape[1]
    group = max(1, 256 // (states * width))
    eye = jnp.eye(group, dtype=F32)
    left_op = left_mpo[0]
    right_op = jnp.transpose(right_mpo[0], (1, 0, 2, 3))
    size = group * states * width
    left_op = parts_outside(jnp.einsum("wvst,gh->vgsthw", left_op, eye, precision="highest").reshape(size, size))
    right_op = parts_outside(jnp.einsum("wvst,gh->tgvwhs", right_op, eye, precision="highest").reshape(size, size))

    row_cuts = shares(rows, (3, 3, 2), group)
    slice_cuts = shares(width, (1, 1, 1, 1), 1)

    pos, left_chunks = 0, []
    for cut in row_cuts:
        left_chunks.append(lax.slice_in_dim(left_e, pos, pos + cut, axis=0))
        pos += cut
    right_w = jnp.transpose(right_e, (1, 0, 2))
    pos, right_chunks = 0, []
    for cut in slice_cuts:
        right_chunks.append(lax.slice_in_dim(right_w, pos, pos + cut, axis=0))
        pos += cut
    left_far = [[moved(c, i=k) for k in range(1, inner)] for c in left_chunks]
    right_far = [[moved(c, o=k) for k in range(1, outer)] for c in right_chunks]

    wide = depth // pair
    left_bra = parts_outside(
        jnp.transpose(lax.dynamic_slice_in_dim(left_t, at_pair * wide, wide, 2), (1, 0, 2))
    )
    right_bra = parts_outside(jnp.transpose(right_t, (1, 0, 2)))

    def block(x, which, axis, start=0, count=rows):
        return lax.dynamic_slice_in_dim(x, which * rows + start, count, axis)

    left_cols = jnp.concatenate(
        [block(left_t, index(at_outer + k, at_inner, at_pair + p), 2) for k in (*range(1, outer), 0) for p in range(pair)],
        2,
    )
    near_rows = min(rows, 32)
    left_order = [
        block(left_cols, index(at_outer, at_inner, at_pair - p), 0, start, near_rows)
        for start in range(0, rows, near_rows)
        for p in range(pair)
    ]
    pos = 0
    for cut in row_cuts:
        for k in range(1, inner):
            for p in range(pair):
                left_order.append(block(left_cols, index(at_outer, at_inner - k, at_pair - p), 0, pos, cut))
        pos += cut
    left_ket = jnp.concatenate(left_order, 0)
    left_ket = parts_outside(jnp.transpose(left_ket, (2, 0, 1)).reshape(left_ket.shape[2], -1))

    right_cols = jnp.concatenate(
        [block(right_t, index(at_outer, at_inner + k, at_pair), 2) for k in (*range(1, inner), 0)], 2
    )
    right_ket = jnp.concatenate(
        [block(right_cols, index(at_outer - k, at_inner, at_pair - p), 0) for k in range(outer) for p in range(pair)],
        0,
    )
    right_ket = parts_outside(jnp.transpose(right_ket, (2, 1, 0)).reshape(-1, right_ket.shape[0]))

    near = [left_e] + [moved(left_e, p=p) for p in range(1, pair)]
    left_pieces = [rows_part(near, near_rows, left_bra, left_op)]
    right_near = [[c] + [moved(c, p=p) for p in range(1, pair)] for c in right_chunks]
    for far in left_far:
        envs = []
        for e in far:
            envs += [e] + [moved(e, p=p) for p in range(1, pair)]
        left_pieces.append(rows_part(envs, envs[0].shape[0], left_bra, left_op))
    right_pieces = []
    for near_c, far in zip(right_near, right_far):
        envs = list(near_c)
        for e in far:
            envs += [e] + [moved(e, p=p) for p in range(1, pair)]
        right_pieces.append(slices_part(envs, right_ket))

    sent = (outer - 1) * pair * rows
    new_left = []
    pos = 0
    for cut in shares(width, (1, 1, 1, 1), 1):
        away, total = close_left(left_pieces, left_ket, pos, cut, sent)
        pos += cut
        for k in range(1, outer):
            total += moved(lax.slice_in_dim(away, (k - 1) * pair * rows, k * pair * rows, axis=1), o=k)
        new_left.append(
            [handed(lax.slice_in_dim(total, p * rows, (p + 1) * rows, axis=1), 1, p) for p in range(pair)]
        )
    new_right = []
    piece = max(group, rows // 4)
    for start in range(0, rows, piece):
        total = close_right(right_pieces, right_op, right_bra, (inner - 1) * rows + start, piece, width)
        for k in range(1, inner):
            out = close_right(right_pieces, right_op, right_bra, (k - 1) * rows + start, piece, width)
            total += moved(out, i=k)
        new_right.append(handed(total, -1))

    segment = lax.axis_index("site")
    last_segment = lax.axis_size("site") - 1
    halves = [jnp.concatenate([piece[p] for piece in new_left], 0) for p in range(pair)]
    ordered = [lax.select_n(((at_pair - q) % pair).astype(jnp.int32) == 0, halves[-1], halves[0]) for q in range(pair)] if pair == 2 else halves
    from_left = jnp.transpose(jnp.concatenate(ordered, 2), (1, 0, 2))
    from_right = jnp.concatenate(new_right, 0)
    out_left = jnp.where(segment == 0, left_e, from_left)
    out_right = jnp.where(segment == last_segment, right_e, from_right)
    return (out_left[None], out_right[None])


def solution(mesh):
    return jax.shard_map(
        functools.partial(local, factors(mesh.shape["bond"])),
        mesh=mesh,
        in_specs=(
            P("site", "bond", None, None),
            P("site", "bond", None, None),
            P("site", None, None, None),
            P("site", None, None, None),
            P("site", None, None, None, None),
            P("site", None, None, None, None),
        ),
        out_specs=(P("site", "bond", None, None), P("site", "bond", None, None)),
        check_vma=False,
    )
```

```python
import functools

import jax
import jax.numpy as jnp
from jax import lax
from jax.experimental import pallas as pl
from jax.experimental.pallas import tpu as pltpu
from jax.sharding import PartitionSpec as P

F32 = jnp.float32
BF16 = jnp.bfloat16
VMEM_BYTES = 40 << 20


def factors(n):
    pair = 2 if n % 2 == 0 else 1
    rest = n // pair
    inner = max(d for d in range(1, rest + 1) if rest % d == 0 and d * d <= rest)
    return rest // inner, inner, pair


def shares(total, weights, unit):
    cuts, done, seen = [], 0, 0
    for weight in weights:
        seen += weight
        upto = (total * seen // sum(weights)) // unit * unit
        cuts.append(upto - done)
        done = upto
    cuts[-1] += total - done
    return [c for c in cuts if c]


def parts(x):
    high = x.astype(BF16)
    return high, (x - high.astype(F32)).astype(BF16)


def parts_outside(x):
    high = lax.reduce_precision(x, 8, 7)
    return high.astype(BF16), (x - high).astype(BF16)


def stacked_parts(x, span):
    rows, columns = x.shape
    high = x.astype(BF16).astype(F32)
    both = [y.reshape(rows // span, span, columns) for y in (high, x - high)]
    return jnp.concatenate(both, 1).reshape(2 * rows, columns).astype(BF16)


def dot(a, b):
    return jnp.dot(a, b, preferred_element_type=F32)


def dot_parts(ah, al, bh, bl):
    return dot(ah, bh) + (dot(ah, bl) + dot(al, bh))


def nothing(*_):
    pass


class Turns:
    def __init__(self):
        self.token = None

    def call(self, body, name, grid, ins, outs, operands, scalars=None, scratch=(), aliases=None, flops=1000, after=()):
        lead = 0 if scalars is None else 1
        waits = [] if self.token is None else [self.token]
        tokens = len(waits)
        waits += after
        token = like((8, 128), F32)
        skip = lead + len(waits)
        count = len(operands) + len(outs)

        def inner(*refs):
            refs[skip + count][...] = jnp.zeros((8, 128), F32)
            body(*refs[:lead], *refs[skip : skip + count], *refs[skip + count + 1 :])

        *results, self.token = pl.pallas_call(
            inner,
            name=name,
            grid_spec=pltpu.PrefetchScalarGridSpec(
                num_scalar_prefetch=lead,
                grid=grid,
                in_specs=[whole(x) for x in waits[:tokens]] + [pl.BlockSpec(memory_space=pl.ANY)] * len(after) + list(ins),
                out_specs=[x for x, _ in outs] + [whole(token)],
                scratch_shapes=list(scratch),
            ),
            out_shape=[x for _, x in outs] + [token],
            input_output_aliases={skip + i: o for i, o in (aliases or {}).items()},
            compiler_params=pltpu.CompilerParams(vmem_limit_bytes=VMEM_BYTES),
            cost_estimate=pl.CostEstimate(flops=flops, bytes_accessed=1000, transcendentals=0),
        )(*([] if scalars is None else [scalars]), *waits, *operands)
        return results


    def take(self, *arrays):
        spec = pl.BlockSpec(memory_space=pl.ANY)
        outs = [(spec, pltpu.HBM(x.shape, x.dtype)) for x in arrays]
        same = {i: i for i in range(len(arrays))}
        return self.call(nothing, "take", (1,), [spec] * len(arrays), outs, [in_hbm(x) for x in arrays], aliases=same)


def whole(x):
    zeros = (0,) * len(x.shape)
    return pl.BlockSpec(tuple(x.shape), lambda *_: zeros)


def like(shape, dtype):
    return jax.ShapeDtypeStruct(tuple(shape), dtype)


def in_hbm(x):
    return pltpu.with_memory_space_constraint(x, pltpu.HBM)


def ids(dims, axis):
    return lax.broadcasted_iota(jnp.int32, dims, axis)


def cut_kernel(*refs):
    half = len(refs) // 2
    for x, out in zip(refs[:half], refs[half:]):
        out[...] = x[...]


def cut_columns(turns, envs, start, wide):
    rows, width, _ = envs[0].shape
    spec = pl.BlockSpec((rows, width, wide), lambda i: (0, 0, start // wide))
    outs = [like((rows, width, wide), F32) for _ in envs]
    return turns.call(cut_kernel, "cut_columns", (1,), [spec] * len(envs), [(whole(o), o) for o in outs], envs)


def operator_kernel(dims, op, out):
    t, v, w, s, g = dims
    rows, columns = t * g * v, w * 2 * g * s
    row, at = ids((rows, t * v), 0), ids((rows, t * v), 1)
    spread = (row // (g * v) * v + row % v == at).astype(F32).astype(BF16)
    at, column = ids((w * s, columns), 0), ids((w * s, columns), 1)
    along = (column // (2 * g * s) * s + column % s == at).astype(F32).astype(BF16)
    row, column = ids((rows, columns), 0), ids((rows, columns), 1)
    same = row // v % g == column // s % g
    low_rows = column // (g * s) % 2 == 1
    high, low = (dot(dot(spread, part).astype(BF16), along) for part in parts(op[...]))
    out[:rows] = jnp.where(same, high, 0.0).astype(BF16)
    out[rows:] = jnp.where(same, jnp.where(low_rows, 0.0, low), 0.0).astype(BF16)


def block_operator(turns, op, dims):
    t, v, w, s, g = dims
    out = like((2 * t * g * v, 2 * w * g * s), BF16)
    return turns.call(
        functools.partial(operator_kernel, dims), "operator", (1,), [whole(op)], [(whole(out), out)], [op]
    )[0]


def bra_kernel(tensor, high, low):
    step, states, _ = tensor.shape
    span = min(step, 32)
    row, at = ids((span * states, span * states), 0), ids((span * states, span * states), 1)
    order = (row % span * states + row // span == at).astype(F32).astype(BF16)
    for start in range(0, step, span):
        x = tensor[start : start + span].reshape(span * states, -1)
        for part, out in zip(parts(x), (high, low)):
            y = dot(order, part).astype(BF16)
            for t in range(states):
                out[t, start : start + span] = y[t * span : (t + 1) * span]


def bra(turns, tensor, after):
    depth, states, wide = tensor.shape
    step = min(depth, 128)
    out = like((states, depth, wide), BF16)
    spec = pl.BlockSpec((states, step, wide), lambda i: (0, i, 0))
    return turns.call(
        bra_kernel,
        "bra",
        (depth // step,),
        [pl.BlockSpec((step, states, wide), lambda i: (i, 0, 0))],
        [(spec, out)] * 2,
        [in_hbm(tensor)],
        after=after,
    )


def ket_kernel(at, *refs):
    tensors, (high, low, turned, mixed) = refs[:-4], refs[-4:]
    rows, states, _ = tensors[0].shape
    start = pl.multiple_of(at[0] * rows, rows)
    for s in range(states):
        turned[...] = jnp.concatenate([tensor[:, s, :] for tensor in tensors], 0).T
        for j in range(mixed.shape[0]):
            mixed[j, pl.ds(s, rows, stride=states), :] = turned[pl.ds(start, rows), j * 128 : (j + 1) * 128]
    for j in range(mixed.shape[0]):
        to = slice(j * 128, (j + 1) * 128)
        high[:, to], low[:, to] = parts(mixed[j])


def ket(turns, tensor, rows, lanes, scalars, row_at, count, lane_at, blocks, after):
    states = tensor.shape[1]
    if lanes % 128 or rows % 8 or count * rows % 128:
        flat = [lax.dynamic_slice_in_dim(tensor, scalars[row_at + q] * rows, rows, 0) for q in range(count)]
        flat = jnp.concatenate(flat, 0)
        starts = [scalars[lane_at + j] * lanes + scalars[0] * rows for j in range(blocks)]
        flat = jnp.concatenate([lax.dynamic_slice_in_dim(flat, b, rows, 2) for b in starts], 2)
        return parts_outside(jnp.transpose(flat, (2, 1, 0)).reshape(-1, flat.shape[0]))

    def spec(q):
        return pl.BlockSpec((rows, states, lanes), lambda j, at: (at[row_at + q], 0, at[lane_at + j]))

    block = (rows * states, count * rows)
    out = (pl.BlockSpec(block, lambda j, _: (j, 0)), like((blocks * block[0], block[1]), BF16))
    return turns.call(
        ket_kernel,
        "ket",
        (blocks,),
        [spec(q) for q in range(count)],
        [out] * 2,
        [in_hbm(tensor)] * count,
        scalars,
        [pltpu.VMEM((lanes, count * rows), F32), pltpu.VMEM((count * rows // 128, rows * states, 128), F32)],
        after=after,
    )


def first_kernel(n, *refs):
    envs, (sh, sl, op, yh, yl, held) = refs[:n], refs[n:]
    width, rows, wide = held.shape
    states = yh.shape[0]
    span = op.shape[1] // width // 2
    at_once = max(1, 512 // wide)

    @pl.when(pl.program_id(0) == 0)
    def _():
        for start in range(0, width, at_once):
            ws = range(start, min(width, start + at_once))
            sides = [jnp.concatenate([env[:, w, :] for env in envs], 0) for w in ws]
            eh, el = parts(jnp.concatenate(sides, 1))
            both = stacked_parts(dot_parts(sh[...], sl[...], eh, el), span)
            for j, w in enumerate(ws):
                held[w] = both[:, j * wide : (j + 1) * wide]

    groups = yh.shape[1] * states // (op.shape[0] // 2)
    base = pl.program_id(0) * groups
    for start in range(0, groups, at_once):
        gs = range(start, min(groups, start + at_once))
        sides = []
        for g in gs:
            at = pl.ds(pl.multiple_of((base + g) * 2 * span, 2 * span), 2 * span)
            sides.append(jnp.concatenate([held[w, at, :] for w in range(width)], 0))
        out = dot(op[...], jnp.concatenate(sides, 1))
        half = out.shape[0] // 2
        h, l = parts(out[:half] + out[half:])
        size = half // states
        for j, g in enumerate(gs):
            for t in range(states):
                to = slice(g * size, (g + 1) * size)
                yh[t, to] = h[t * size : (t + 1) * size, j * wide : (j + 1) * wide]
                yl[t, to] = l[t * size : (t + 1) * size, j * wide : (j + 1) * wide]


def first_part(turns, near, far, start, wide, ket, op, states, b_at, b_count):
    rows, width, _ = near[0].shape
    made, depth = b_count * states, ket[0].shape[1]
    steps = 4
    out = pltpu.HBM((states, made // states * width, wide), BF16)
    spec = pl.BlockSpec((states, out.shape[1] // steps, wide), lambda i: (0, i, 0))
    near_spec = pl.BlockSpec((rows, width, wide), lambda i: (0, 0, start // wide))
    ket_spec = pl.BlockSpec((made, depth), lambda i: (b_at // b_count, 0))
    h, l = turns.call(
        functools.partial(first_kernel, len(near) + len(far)),
        "first_part",
        (steps,),
        [near_spec] * len(near) + [whole(x) for x in far] + [ket_spec] * 2 + [whole(op)],
        [(spec, out)] * 2,
        [*near, *far, *ket, op],
        scratch=[pltpu.VMEM((width, 2 * made, wide), BF16)],
    )
    return h, l, b_at


def second_kernel(n, *refs):
    yhs, yls, (sh, sl), more, out = refs[:n], refs[n : 2 * n], refs[2 * n : 2 * n + 2], refs[2 * n + 2 : -1], refs[-1]
    states, depth, columns = sh.shape
    row = lambda ys: jnp.concatenate([y[t] for t in range(states) for y in ys], 1)
    flat = lambda s: s[...].reshape(states * depth, columns)
    total = dot_parts(row(yhs), row(yls), flat(sh), flat(sl)).reshape(out.shape)
    for x in more:
        total += x[...]
    out[...] = total


def second_part(turns, pieces, bra, start, count, width, more):
    states, depth, columns = bra[0].shape
    pieces = [p for p in pieces if p[2] <= start < p[2] + p[0].shape[1] // width]
    yhs = [in_hbm(h) for h, _, _ in pieces]
    yls = [in_hbm(l) for _, l, _ in pieces]
    block = next(b for b in range(min(count, 16), 0, -1) if start % b == 0 and count % b == 0)

    def y_spec(y, base):
        return pl.BlockSpec((states, block * width, y.shape[2]), lambda i: (0, (start - base) // block + i, 0))

    spec = pl.BlockSpec((block, width, columns), lambda i: (i, 0, 0))
    return turns.call(
        functools.partial(second_kernel, len(pieces)),
        "second_part",
        (count // block,),
        [y_spec(y, base) for y, (_, _, base) in zip((*yhs, *yls), pieces * 2)] + [whole(x) for x in bra] + [spec] * len(more),
        [(spec, like((count, width, columns), F32))],
        [*yhs, *yls, *bra, *more],
    )[0]


def place_kernel(edge, start, old, at, piece, env, *refs):
    out, held, arrived = refs[old], refs[old + 1], refs[old + 2]
    rows = pl.ds(start, piece.shape[0])

    def through(source, target):
        copy = pltpu.make_async_copy(source, target, arrived)
        copy.start()
        copy.wait()

    @pl.when(at[1] == edge)
    def _():
        through(env.at[rows], held)

    @pl.when(at[1] != edge)
    def _():
        through(piece, held)

    through(held, out.at[rows])


def place(turns, piece, env, start, old, scalars, edge):
    spec = pl.BlockSpec(memory_space=pl.ANY)
    return turns.call(
        functools.partial(place_kernel, edge, start, len(old)),
        "place",
        (1,),
        [spec] * (2 + len(old)),
        [(spec, pltpu.HBM(env.shape, F32))],
        [piece, env, *map(in_hbm, old)],
        scalars,
        [pltpu.VMEM(piece.shape, F32), pltpu.SemaphoreType.DMA(())],
        aliases={2 + i: i for i in range(len(old))},
    )


def local(sizes, left_env, right_env, left_site, right_site, left_mpo, right_mpo):
    outer, inner, pair = sizes
    n = outer * inner * pair
    chain = lax.axis_size("site")
    index = lambda o, i, p: (o % outer * inner + i % inner) * pair + p % pair

    def moved(x, o=0, i=0, p=0):
        route = []
        for d in range(n):
            do, di, dp = d // (inner * pair), d // pair % inner, d % pair
            route.append((d, index(do + o, di + i, dp + p)))
        return lax.ppermute(x, "bond", route)

    def handed(x, distance):
        return lax.ppermute(x, "site", [(k, k + distance) for k in range(chain) if 0 <= k + distance < chain])

    table = []
    for k in range(chain):
        for d in range(n):
            o, i, p = d // (inner * pair), d // pair % inner, d % pair
            left_rows = [index(o, i - k, p - q) for k in range(inner) for q in range(pair)]
            left_lanes = [index(o + k, i, 0) // pair for k in (*range(1, outer), 0)]
            right_rows = [index(o - k, i, p - q) for k in range(outer) for q in range(pair)]
            right_lanes = [index(o, i + k, 0) // pair for k in (*range(1, inner), 0)]
            table.append([p, k, *left_rows, *left_lanes, *right_rows, *right_lanes])
    scalars = jnp.asarray(table, jnp.int32)[lax.axis_index(("site", "bond"))]

    rows, width, depth = left_env.shape[1:]
    states = left_site.shape[2]
    group = max(1, 128 // (states * width))
    dims = (states, width, width, states, group)
    lane = 128 if depth % 128 == 0 else depth
    cuts = shares(depth, (1, 1), lane)
    pieces = shares(rows, (1, 1), group)

    class Side:
        def __init__(self, env, tensor, op, gather, reduce, row_at, distance):
            self.env, self.tensor, self.op = in_hbm(env[0]), tensor[0], op
            self.gather, self.reduce, self.row_at, self.distance = gather, reduce, row_at, distance
            self.ranks = {"o": outer, "i": inner}[gather]
            self.others = {"o": outer, "i": inner}[reduce]
            self.done, self.sent, self.handed, self.out = [], [], [], []

        def gather_near(self):
            self.near = [self.env] + [moved(self.env, p=p) for p in range(1, pair)]

        def gather_far(self, x):
            return [moved(x, **{self.gather: k}) for k in range(1, self.ranks)]

        def share(self, far):
            return [y for x in far for y in [x] + [moved(x, p=p) for p in range(1, pair)]]

        def prepare(self, after):
            count = self.ranks * pair
            self.operator = block_operator(turns, self.op, dims)
            self.ket = ket(
                turns, self.tensor, rows, pair * rows, scalars, self.row_at, count, self.row_at + count, self.others, after
            )

        def prepare_bra(self, after):
            self.bra = bra(turns, self.tensor, after)

        def first(self, j, far, b_at, b_count):
            args = self.near, far, sum(cuts[:j]), cuts[j], self.ket, self.operator, states
            self.done.append(first_part(turns, *args, b_at, b_count))

        def send(self, j):
            got = []
            for k in range(1, self.others):
                start = (k - 1) * rows + sum(pieces[:j])
                x = second_part(turns, self.done, self.bra, start, pieces[j], width, [])
                got.append(moved(x, **{self.reduce: k}))
            self.sent.append(got)

        def keep(self, j):
            start = (self.others - 1) * rows + sum(pieces[:j])
            x = second_part(turns, self.done, self.bra, start, pieces[j], width, self.sent[j])
            self.handed.append(handed(x, self.distance))

        def place(self, j):
            edge = 0 if self.distance > 0 else chain - 1
            self.out = place(turns, self.handed[j], self.env, sum(pieces[:j]), self.out, scalars, edge)

    turns = Turns()
    left_op = jnp.transpose(left_mpo[0], (3, 1, 0, 2)).reshape(states * width, -1)
    right_op = jnp.transpose(right_mpo[0], (3, 0, 1, 2)).reshape(states * width, -1)
    left = Side(left_env, left_site, left_op, "i", "o", 2, 1)
    right = Side(right_env, right_site, right_op, "o", "i", 2 + inner * pair + outer, -1)
    both = (left, right)

    far = {}

    def gather(j):
        chunks = cut_columns(turns, [side.env for side in both], sum(cuts[:j]), cuts[j])
        for side, x in zip(both, chunks):
            far[side, j] = side.gather_far(x)

    def share(j):
        arrived = turns.take(*far[left, j], *far[right, j])
        count = len(far[left, j])
        far[left, j] = left.share(arrived[:count])
        far[right, j] = right.share(arrived[count:])

    def first(side, j):
        side.first(j, far[side, j], 0, side.others * rows)

    for side in both:
        side.gather_near()
    gather(0)
    left.prepare(left.near[1:] + right.near[1:])
    right.prepare([])
    last = len(cuts) - 1
    for j in range(1, last + 1):
        gather(j)
    for side in both:
        side.prepare_bra([])
    for j in range(last + 1):
        share(j)
        for side in both:
            first(side, j)
            if j == last:
                side.send(0)
    for j in range(1, len(pieces)):
        for side in both:
            side.send(j)
    for j in range(len(pieces)):
        for side in both:
            side.keep(j)
    for j in range(len(pieces)):
        for side in both:
            side.place(j)
    return (left.out[0][None], right.out[0][None])


def solution(mesh):
    return jax.shard_map(
        functools.partial(local, factors(mesh.shape["bond"])),
        mesh=mesh,
        in_specs=(
            P("site", "bond", None, None),
            P("site", "bond", None, None),
            P("site", None, None, None),
            P("site", None, None, None),
            P("site", None, None, None, None),
            P("site", None, None, None, None),
        ),
        out_specs=(P("site", "bond", None, None), P("site", "bond", None, None)),
        check_vma=False,
    )
```

```python
import functools

import jax
import jax.numpy as jnp
from jax import lax
from jax.experimental import pallas as pl
from jax.experimental.pallas import tpu as pltpu
from jax.sharding import PartitionSpec as P

F32 = jnp.float32
BF16 = jnp.bfloat16
VMEM_BYTES = 27 << 20
FLOPS_A_US = 10**11


def factors(n):
    pair = 2 if n % 2 == 0 else 1
    rest = n // pair
    inner = max(d for d in range(1, rest + 1) if rest % d == 0 and d * d <= rest)
    return rest // inner, inner, pair


def shares(total, weights, unit):
    cuts, done, seen = [], 0, 0
    for weight in weights:
        seen += weight
        upto = (total * seen // sum(weights)) // unit * unit
        cuts.append(upto - done)
        done = upto
    cuts[-1] += total - done
    return [c for c in cuts if c]


def parts(x):
    high = x.astype(BF16)
    return high, (x - high.astype(F32)).astype(BF16)


def parts_outside(x):
    high = lax.reduce_precision(x, 8, 7)
    return high.astype(BF16), (x - high).astype(BF16)


def stacked_parts(x, span):
    rows, columns = x.shape
    high = x.astype(BF16).astype(F32)
    both = [y.reshape(rows // span, span, columns) for y in (high, x - high)]
    return jnp.concatenate(both, 1).reshape(2 * rows, columns).astype(BF16)


def dot(a, b):
    return jnp.dot(a, b, preferred_element_type=F32)


def dot_parts(ah, al, bh, bl):
    return dot(ah, bh) + (dot(ah, bl) + dot(al, bh))


def nothing(*_):
    pass


class Turns:
    def __init__(self):
        self.token = None

    def call(self, body, name, grid, ins, outs, operands, scalars=None, scratch=(), aliases=None, about_us=0.3, after=()):
        lead = 0 if scalars is None else 1
        waits = [] if self.token is None else [self.token]
        tokens = len(waits)
        waits += after
        token = like((8, 128), F32)
        skip = lead + len(waits)
        count = len(operands) + len(outs)

        def inner(*refs):
            refs[skip + count][...] = jnp.zeros((8, 128), F32)
            body(*refs[:lead], *refs[skip : skip + count], *refs[skip + count + 1 :])

        *results, self.token = pl.pallas_call(
            inner,
            name=name,
            grid_spec=pltpu.PrefetchScalarGridSpec(
                num_scalar_prefetch=lead,
                grid=grid,
                in_specs=[whole(x) for x in waits[:tokens]] + [pl.BlockSpec(memory_space=pl.ANY)] * len(after) + list(ins),
                out_specs=[x for x, _ in outs] + [whole(token)],
                scratch_shapes=list(scratch),
            ),
            out_shape=[x for _, x in outs] + [token],
            input_output_aliases={skip + i: o for i, o in (aliases or {}).items()},
            compiler_params=pltpu.CompilerParams(vmem_limit_bytes=VMEM_BYTES),
            cost_estimate=pl.CostEstimate(flops=int(about_us * FLOPS_A_US), bytes_accessed=1000, transcendentals=0),
        )(*([] if scalars is None else [scalars]), *waits, *operands)
        return results


    def take(self, *arrays):
        spec = pl.BlockSpec(memory_space=pl.ANY)
        outs = [(spec, pltpu.HBM(x.shape, x.dtype)) for x in arrays]
        same = {i: i for i in range(len(arrays))}
        return self.call(nothing, "take", (1,), [spec] * len(arrays), outs, [in_hbm(x) for x in arrays], aliases=same)


def whole(x):
    zeros = (0,) * len(x.shape)
    return pl.BlockSpec(tuple(x.shape), lambda *_: zeros)


def like(shape, dtype):
    return jax.ShapeDtypeStruct(tuple(shape), dtype)


def in_hbm(x):
    return pltpu.with_memory_space_constraint(x, pltpu.HBM)


def ids(dims, axis):
    return lax.broadcasted_iota(jnp.int32, dims, axis)


def cut_kernel(*refs):
    half = len(refs) // 2
    for x, out in zip(refs[:half], refs[half:]):
        for w in range(out.shape[0]):
            out[w] = x[:, w, :]


def cut_columns(turns, envs, start, wide):
    rows, width, _ = envs[0].shape
    spec = pl.BlockSpec((rows, width, wide), lambda i: (0, 0, start // wide))
    out = like((width, rows, wide), F32)
    return turns.call(cut_kernel, "cut_columns", (1,), [spec] * len(envs), [(whole(out), out)] * len(envs), envs)


def operator_kernel(dims, op, out):
    t, v, w, s, g = dims
    rows, columns = t * g * v, w * 2 * g * s
    row, at = ids((rows, t * v), 0), ids((rows, t * v), 1)
    spread = (row // (g * v) * v + row % v == at).astype(F32).astype(BF16)
    at, column = ids((w * s, columns), 0), ids((w * s, columns), 1)
    along = (column // (2 * g * s) * s + column % s == at).astype(F32).astype(BF16)
    row, column = ids((rows, columns), 0), ids((rows, columns), 1)
    same = row // v % g == column // s % g
    low_rows = column // (g * s) % 2 == 1
    high, low = (dot(dot(spread, part).astype(BF16), along) for part in parts(op[...]))
    out[:rows] = jnp.where(same, high, 0.0).astype(BF16)
    out[rows:] = jnp.where(same, jnp.where(low_rows, 0.0, low), 0.0).astype(BF16)


def block_operator(turns, op, dims):
    t, v, w, s, g = dims
    out = like((2 * t * g * v, 2 * w * g * s), BF16)
    return turns.call(
        functools.partial(operator_kernel, dims), "operator", (1,), [whole(op)], [(whole(out), out)], [op]
    )[0]


def bra_kernel(tensor, high, low):
    step, states, _ = tensor.shape
    span = min(step, 32)
    row, at = ids((span * states, span * states), 0), ids((span * states, span * states), 1)
    order = (row % span * states + row // span == at).astype(F32).astype(BF16)
    for start in range(0, step, span):
        x = tensor[start : start + span].reshape(span * states, -1)
        for part, out in zip(parts(x), (high, low)):
            y = dot(order, part).astype(BF16)
            for t in range(states):
                out[t, start : start + span] = y[t * span : (t + 1) * span]


def bra(turns, tensor, after):
    depth, states, wide = tensor.shape
    step = min(depth, 128)
    out = like((states, depth, wide), BF16)
    spec = pl.BlockSpec((states, step, wide), lambda i: (0, i, 0))
    return turns.call(
        bra_kernel,
        "bra",
        (depth // step,),
        [pl.BlockSpec((step, states, wide), lambda i: (i, 0, 0))],
        [(spec, out)] * 2,
        [in_hbm(tensor)],
        after=after,
        about_us=4,
    )


def ket_kernel(at, *refs):
    tensors, (high, low, turned, mixed) = refs[:-4], refs[-4:]
    rows, states, _ = tensors[0].shape
    start = pl.multiple_of(at[0] * rows, rows)
    for s in range(states):
        turned[...] = jnp.concatenate([tensor[:, s, :] for tensor in tensors], 0).T
        for j in range(mixed.shape[0]):
            mixed[j, pl.ds(s, rows, stride=states), :] = turned[pl.ds(start, rows), j * 128 : (j + 1) * 128]
    for j in range(mixed.shape[0]):
        to = slice(j * 128, (j + 1) * 128)
        high[:, to], low[:, to] = parts(mixed[j])


def ket(turns, tensor, rows, lanes, scalars, row_at, count, lane_at, blocks, after):
    states = tensor.shape[1]
    if lanes % 128 or rows % 8 or count * rows % 128:
        flat = [lax.dynamic_slice_in_dim(tensor, scalars[row_at + q] * rows, rows, 0) for q in range(count)]
        flat = jnp.concatenate(flat, 0)
        starts = [scalars[lane_at + j] * lanes + scalars[0] * rows for j in range(blocks)]
        flat = jnp.concatenate([lax.dynamic_slice_in_dim(flat, b, rows, 2) for b in starts], 2)
        return parts_outside(jnp.transpose(flat, (2, 1, 0)).reshape(-1, flat.shape[0]))

    def spec(q):
        return pl.BlockSpec((rows, states, lanes), lambda j, at: (at[row_at + q], 0, at[lane_at + j]))

    block = (rows * states, count * rows)
    out = (pl.BlockSpec(block, lambda j, _: (j, 0)), like((blocks * block[0], block[1]), BF16))
    return turns.call(
        ket_kernel,
        "ket",
        (blocks,),
        [spec(q) for q in range(count)],
        [out] * 2,
        [in_hbm(tensor)] * count,
        scalars,
        [pltpu.VMEM((lanes, count * rows), F32), pltpu.VMEM((count * rows // 128, rows * states, 128), F32)],
        after=after,
        about_us=2.7,
    )


def first_kernel(raw, *refs):
    n = len(raw)
    envs, (sh, sl, op, yh, yl, held) = refs[:n], refs[n:]
    width, _, wide = held.shape
    states = yh.shape[0]
    span = op.shape[1] // width // 2
    at_once = max(1, 512 // wide)

    here = envs[0].shape[0]
    halves = width // here
    step = pl.program_id(0)

    @pl.when(step < halves)
    def _():
        for start in range(0, here, at_once):
            ws = range(start, min(here, start + at_once))
            pick = lambda w: [env[:, w, :] if r else env[w] for r, env in zip(raw, envs)]
            sides = [jnp.concatenate(pick(w), 0) for w in ws]
            eh, el = parts(jnp.concatenate(sides, 1))
            both = stacked_parts(dot_parts(sh[...], sl[...], eh, el), span)
            for j, w in enumerate(ws):
                held[step * here + w] = both[:, j * wide : (j + 1) * wide]

    @pl.when(step >= halves)
    def _():
        groups = yh.shape[1] * states // (op.shape[0] // 2)
        base = (step - halves) * groups
        for start in range(0, groups, at_once):
            gs = range(start, min(groups, start + at_once))
            sides = []
            for g in gs:
                at = pl.ds(pl.multiple_of((base + g) * 2 * span, 2 * span), 2 * span)
                sides.append(jnp.concatenate([held[w, at, :] for w in range(width)], 0))
            out = dot(op[...], jnp.concatenate(sides, 1))
            half = out.shape[0] // 2
            h, l = parts(out[:half] + out[half:])
            size = half // states
            for j, g in enumerate(gs):
                for t in range(states):
                    to = slice(g * size, (g + 1) * size)
                    yh[t, to] = h[t * size : (t + 1) * size, j * wide : (j + 1) * wide]
                    yl[t, to] = l[t * size : (t + 1) * size, j * wide : (j + 1) * wide]


def first_part(turns, own, near, far, start, ket, op, states, b_at, b_count):
    width, rows, wide = own.shape
    made, depth = b_count * states, ket[0].shape[1]
    steps = 4
    shape = (states, made // states * width, wide)
    out = like(shape, BF16) if start else pltpu.HBM(shape, BF16)
    halves = 2 if width % 16 == 0 else 1
    here = width // halves
    spec = pl.BlockSpec((states, out.shape[1] // steps, wide), lambda i: (0, jnp.maximum(i - halves, 0), 0))
    near_spec = pl.BlockSpec((rows, here, wide), lambda i: (0, jnp.minimum(i, halves - 1), start // wide))
    far_spec = pl.BlockSpec((here, rows, wide), lambda i: (jnp.minimum(i, halves - 1), 0, 0))
    ket_spec = pl.BlockSpec((made, depth), lambda i: (b_at // b_count, 0))
    h, l = turns.call(
        functools.partial(first_kernel, (False, *(True for _ in near), *(False for _ in far))),
        "first_part",
        (halves + steps,),
        [far_spec] + [near_spec] * len(near) + [far_spec] * len(far) + [ket_spec] * 2 + [whole(op)],
        [(spec, out)] * 2,
        [own, *near, *far, *ket, op],
        scratch=[pltpu.VMEM((width, 2 * made, wide), BF16)],
        about_us=3 + 0.03 * wide,
    )
    return (h, l, b_at) if start else (in_hbm(h), in_hbm(l), b_at)


def second_kernel(n, *refs):
    yhs, yls, (sh, sl), more, out = refs[:n], refs[n : 2 * n], refs[2 * n : 2 * n + 2], refs[2 * n + 2 : -1], refs[-1]
    row = lambda ys: jnp.concatenate([y[t] for t in range(ys[0].shape[0]) for y in ys], 1)
    flat = lambda s: s[...].reshape(-1, s.shape[2])
    total = dot_parts(row(yhs), row(yls), flat(sh), flat(sl)).reshape(out.shape)
    for x in more:
        total += x[...]
    out[...] = total


def second_part(turns, pieces, bra, start, count, width, more):
    states, depth, columns = bra[0].shape
    pieces = [p for p in pieces if p[2] <= start < p[2] + p[0].shape[1] // width]
    yhs = [h for h, _, _ in pieces]
    yls = [l for _, l, _ in pieces]
    block = next(b for b in range(min(count, 24), 0, -1) if start % b == 0 and count % b == 0)

    def y_spec(y, base):
        return pl.BlockSpec((states, block * width, y.shape[2]), lambda i: (0, (start - base) // block + i, 0))

    spec = pl.BlockSpec((block, width, columns), lambda i: (i, 0, 0))
    return turns.call(
        functools.partial(second_kernel, len(pieces)),
        "second_part",
        (count // block,),
        [y_spec(y, base) for y, (_, _, base) in zip((*yhs, *yls), pieces * 2)] + [whole(x) for x in bra] + [spec] * len(more),
        [(spec, like((count, width, columns), F32))],
        [*yhs, *yls, *bra, *more],
        about_us=3e-2,
    )[0]


def place_kernel(edge, start, old, at, piece, env, *refs):
    out, held, arrived = refs[old], refs[old + 1], refs[old + 2]
    rows = pl.ds(start, piece.shape[0])

    def through(source, target):
        copy = pltpu.make_async_copy(source, target, arrived)
        copy.start()
        copy.wait()

    @pl.when(at[1] == edge)
    def _():
        through(env.at[rows], held)

    @pl.when(at[1] != edge)
    def _():
        through(piece, held)

    through(held, out.at[rows])


def place(turns, piece, env, start, old, scalars, edge):
    spec = pl.BlockSpec(memory_space=pl.ANY)
    return turns.call(
        functools.partial(place_kernel, edge, start, len(old)),
        "place",
        (1,),
        [spec] * (2 + len(old)),
        [(spec, pltpu.HBM(env.shape, F32))],
        [piece, env, *map(in_hbm, old)],
        scalars,
        [pltpu.VMEM(piece.shape, F32), pltpu.SemaphoreType.DMA(())],
        aliases={2 + i: i for i in range(len(old))},
        about_us=1e-1,
    )


def local(sizes, left_env, right_env, left_site, right_site, left_mpo, right_mpo):
    outer, inner, pair = sizes
    n = outer * inner * pair
    chain = lax.axis_size("site")
    index = lambda o, i, p: (o % outer * inner + i % inner) * pair + p % pair

    def moved(x, o=0, i=0, p=0):
        route = []
        for d in range(n):
            do, di, dp = d // (inner * pair), d // pair % inner, d % pair
            route.append((d, index(do + o, di + i, dp + p)))
        return lax.ppermute(x, "bond", route)

    def handed(x, distance):
        return lax.ppermute(x, "site", [(k, k + distance) for k in range(chain) if 0 <= k + distance < chain])

    table = []
    for k in range(chain):
        for d in range(n):
            o, i, p = d // (inner * pair), d // pair % inner, d % pair
            left_rows = [index(o, i - k, p - q) for k in range(inner) for q in range(pair)]
            left_lanes = [index(o + k, i, 0) // pair for k in (*range(1, outer), 0)]
            right_rows = [index(o - k, i, p - q) for k in range(outer) for q in range(pair)]
            right_lanes = [index(o, i + k, 0) // pair for k in (*range(1, inner), 0)]
            table.append([p, k, *left_rows, *left_lanes, *right_rows, *right_lanes])
    scalars = jnp.asarray(table, jnp.int32)[lax.axis_index(("site", "bond"))]

    rows, width, depth = left_env.shape[1:]
    states = left_site.shape[2]
    group = max(1, 128 // (states * width))
    dims = (states, width, width, states, group)
    lane = 128 if depth % 128 == 0 else depth
    cuts = shares(depth, (1, 1), lane)

    class Side:
        def __init__(self, env, tensor, op, gather, reduce, row_at, distance):
            self.env, self.tensor, self.op = in_hbm(env[0]), tensor[0], op
            self.gather, self.reduce, self.row_at, self.distance = gather, reduce, row_at, distance
            self.ranks = {"o": outer, "i": inner}[gather]
            self.others = {"o": outer, "i": inner}[reduce]
            self.pieces = shares(rows, (1, 1) if distance > 0 else (2, 3, 3), group)
            self.own, self.done, self.sent, self.handed, self.out = [], [], [], [], []

        def gather_near(self):
            self.near = [moved(self.env, p=p) for p in range(1, pair)]

        def gather_far(self, x):
            return [moved(x, **{self.gather: k}) for k in range(1, self.ranks)]

        def share(self, far):
            return [y for x in far for y in [x] + [moved(x, p=p) for p in range(1, pair)]]

        def prepare(self, after):
            count = self.ranks * pair
            self.operator = block_operator(turns, self.op, dims)
            self.ket = ket(
                turns, self.tensor, rows, pair * rows, scalars, self.row_at, count, self.row_at + count, self.others, after
            )

        def prepare_bra(self, after):
            self.bra = bra(turns, self.tensor, after)

        def first(self, j, far, b_at, b_count):
            args = self.own[j], self.near, far, sum(cuts[:j]), self.ket, self.operator, states
            self.done.append(first_part(turns, *args, b_at, b_count))

        def send(self, j):
            got = []
            for k in range(1, self.others):
                start = (k - 1) * rows + sum(self.pieces[:j])
                x = second_part(turns, self.done, self.bra, start, self.pieces[j], width, [])
                got.append(moved(x, **{self.reduce: k}))
            self.sent.append(got)

        def keep(self, j):
            start = (self.others - 1) * rows + sum(self.pieces[:j])
            x = second_part(turns, self.done, self.bra, start, self.pieces[j], width, self.sent[j])
            self.handed.append(handed(x, self.distance))

        def place(self, j):
            edge = 0 if self.distance > 0 else chain - 1
            self.out = place(turns, self.handed[j], self.env, sum(self.pieces[:j]), self.out, scalars, edge)

    turns = Turns()
    left_op = jnp.transpose(left_mpo[0], (3, 1, 0, 2)).reshape(states * width, -1)
    right_op = jnp.transpose(right_mpo[0], (3, 0, 1, 2)).reshape(states * width, -1)
    left = Side(left_env, left_site, left_op, "i", "o", 2, 1)
    right = Side(right_env, right_site, right_op, "o", "i", 2 + inner * pair + outer, -1)
    both = (left, right)

    far = {}

    def gather(j):
        chunks = cut_columns(turns, [side.env for side in both], sum(cuts[:j]), cuts[j])
        for side, x in zip(both, chunks):
            side.own.append(x)
            far[side, j] = side.gather_far(x)

    def share(j):
        arrived = [*far[left, j], *far[right, j]]
        arrived = turns.take(*arrived)
        count = len(far[left, j])
        far[left, j] = left.share(arrived[:count])
        far[right, j] = right.share(arrived[count:])

    def first(side, j):
        side.first(j, far[side, j], 0, side.others * rows)

    for side in both:
        side.gather_near()
    gather(0)
    left.prepare(left.near + right.near)
    right.prepare([])
    gather(1)
    for side in both:
        side.prepare_bra([])
    share(0)
    first(left, 0)
    first(right, 0)
    share(1)
    first(left, 1)
    left.send(0)
    first(right, 1)
    right.send(0)
    left.send(1)
    right.send(1)
    left.keep(0)
    right.keep(0)
    right.send(2)
    right.keep(1)
    left.keep(1)
    left.place(0)
    right.place(0)
    right.keep(2)
    right.place(1)
    left.place(1)
    right.place(2)
    return (left.out[0][None], right.out[0][None])


def solution(mesh):
    return jax.shard_map(
        functools.partial(local, factors(mesh.shape["bond"])),
        mesh=mesh,
        in_specs=(
            P("site", "bond", None, None),
            P("site", "bond", None, None),
            P("site", None, None, None),
            P("site", None, None, None),
            P("site", None, None, None, None),
            P("site", None, None, None, None),
        ),
        out_specs=(P("site", "bond", None, None), P("site", "bond", None, None)),
        check_vma=False,
    )
```

```python
import functools

import jax
import jax.numpy as jnp
from jax import lax
from jax.experimental import pallas as pl
from jax.experimental.pallas import tpu as pltpu
from jax.sharding import PartitionSpec as P

F32 = jnp.float32
BF16 = jnp.bfloat16
VMEM_BYTES = 22 << 20
FLOPS_A_US = 10**11


def factors(n):
    pair = 2 if n % 2 == 0 else 1
    rest = n // pair
    inner = max(d for d in range(1, rest + 1) if rest % d == 0 and d * d <= rest)
    return rest // inner, inner, pair


def shares(total, weights, unit):
    cuts, done, seen = [], 0, 0
    for weight in weights:
        seen += weight
        upto = (total * seen // sum(weights)) // unit * unit
        cuts.append(upto - done)
        done = upto
    cuts[-1] += total - done
    return [c for c in cuts if c]


def parts(x):
    high = x.astype(BF16)
    return high, (x - high.astype(F32)).astype(BF16)


def parts_outside(x):
    high = lax.reduce_precision(x, 8, 7)
    return high.astype(BF16), (x - high).astype(BF16)


def stacked_parts(x, span):
    rows, columns = x.shape
    high = x.astype(BF16).astype(F32)
    both = [y.reshape(rows // span, span, columns) for y in (high, x - high)]
    return jnp.concatenate(both, 1).reshape(2 * rows, columns).astype(BF16)


def dot(a, b):
    return jnp.dot(a, b, preferred_element_type=F32)


def dot_parts(ah, al, bh, bl):
    return dot(ah, bh) + (dot(ah, bl) + dot(al, bh))


def nothing(*_):
    pass


class Turns:
    def __init__(self):
        self.token = None

    def call(self, body, name, grid, ins, outs, operands, scalars=None, scratch=(), aliases=None, about_us=0.3, after=()):
        lead = 0 if scalars is None else 1
        waits = [] if self.token is None else [self.token]
        tokens = len(waits)
        waits += after
        token = like((8, 128), F32)
        skip = lead + len(waits)
        count = len(operands) + len(outs)

        def inner(*refs):
            refs[skip + count][...] = jnp.zeros((8, 128), F32)
            body(*refs[:lead], *refs[skip : skip + count], *refs[skip + count + 1 :])

        *results, self.token = pl.pallas_call(
            inner,
            name=name,
            grid_spec=pltpu.PrefetchScalarGridSpec(
                num_scalar_prefetch=lead,
                grid=grid,
                in_specs=[whole(x) for x in waits[:tokens]] + [pl.BlockSpec(memory_space=pl.ANY)] * len(after) + list(ins),
                out_specs=[x for x, _ in outs] + [whole(token)],
                scratch_shapes=list(scratch),
            ),
            out_shape=[x for _, x in outs] + [token],
            input_output_aliases={skip + i: o for i, o in (aliases or {}).items()},
            compiler_params=pltpu.CompilerParams(vmem_limit_bytes=VMEM_BYTES),
            cost_estimate=pl.CostEstimate(flops=int(about_us * FLOPS_A_US), bytes_accessed=1000, transcendentals=0),
        )(*([] if scalars is None else [scalars]), *waits, *operands)
        return results


    def take(self, *arrays):
        spec = pl.BlockSpec(memory_space=pl.ANY)
        outs = [(spec, pltpu.HBM(x.shape, x.dtype)) for x in arrays]
        same = {i: i for i in range(len(arrays))}
        return self.call(nothing, "take", (1,), [spec] * len(arrays), outs, [in_hbm(x) for x in arrays], aliases=same)


def whole(x):
    zeros = (0,) * len(x.shape)
    return pl.BlockSpec(tuple(x.shape), lambda *_: zeros)


def like(shape, dtype):
    return jax.ShapeDtypeStruct(tuple(shape), dtype)


def in_hbm(x):
    return pltpu.with_memory_space_constraint(x, pltpu.HBM)


def ids(dims, axis):
    return lax.broadcasted_iota(jnp.int32, dims, axis)


def cut_kernel(*refs):
    half = len(refs) // 2
    for x, out in zip(refs[:half], refs[half:]):
        for w in range(out.shape[0]):
            out[w] = x[:, w, :]


def cut_columns(turns, envs, start, wide):
    rows, width, _ = envs[0].shape
    spec = pl.BlockSpec((rows, width, wide), lambda i: (0, 0, start // wide))
    out = like((width, rows, wide), F32)
    return turns.call(cut_kernel, "cut_columns", (1,), [spec] * len(envs), [(whole(out), out)] * len(envs), envs)


def operator_kernel(dims, op, out):
    t, v, w, s, g = dims
    rows, columns = t * g * v, w * 2 * g * s
    row, at = ids((rows, t * v), 0), ids((rows, t * v), 1)
    spread = (row // (g * v) * v + row % v == at).astype(F32).astype(BF16)
    at, column = ids((w * s, columns), 0), ids((w * s, columns), 1)
    along = (column // (2 * g * s) * s + column % s == at).astype(F32).astype(BF16)
    row, column = ids((rows, columns), 0), ids((rows, columns), 1)
    same = row // v % g == column // s % g
    low_rows = column // (g * s) % 2 == 1
    high, low = (dot(dot(spread, part).astype(BF16), along) for part in parts(op[...]))
    out[:rows] = jnp.where(same, high, 0.0).astype(BF16)
    out[rows:] = jnp.where(same, jnp.where(low_rows, 0.0, low), 0.0).astype(BF16)


def block_operator(turns, op, dims):
    t, v, w, s, g = dims
    out = like((2 * t * g * v, 2 * w * g * s), BF16)
    return turns.call(
        functools.partial(operator_kernel, dims), "operator", (1,), [whole(op)], [(whole(out), out)], [op]
    )[0]


def bra_kernel(tensor, high, low):
    step, states, _ = tensor.shape
    span = min(step, 32)
    row, at = ids((span * states, span * states), 0), ids((span * states, span * states), 1)
    order = (row % span * states + row // span == at).astype(F32).astype(BF16)
    for start in range(0, step, span):
        x = tensor[start : start + span].reshape(span * states, -1)
        for part, out in zip(parts(x), (high, low)):
            y = dot(order, part).astype(BF16)
            for t in range(states):
                out[t, start : start + span] = y[t * span : (t + 1) * span]


def bra(turns, tensor, after):
    depth, states, wide = tensor.shape
    step = min(depth, 128)
    out = like((states, depth, wide), BF16)
    spec = pl.BlockSpec((states, step, wide), lambda i: (0, i, 0))
    return turns.call(
        bra_kernel,
        "bra",
        (depth // step,),
        [pl.BlockSpec((step, states, wide), lambda i: (i, 0, 0))],
        [(spec, out)] * 2,
        [tensor],
        after=after,
        about_us=4,
    )


def ket_kernel(at, *refs):
    tensors, (high, low, turned, mixed) = refs[:-4], refs[-4:]
    rows, states, _ = tensors[0].shape
    start = pl.multiple_of(at[0] * rows, rows)
    for s in range(states):
        turned[...] = jnp.concatenate([tensor[:, s, :] for tensor in tensors], 0).T
        for j in range(mixed.shape[0]):
            mixed[j, pl.ds(s, rows, stride=states), :] = turned[pl.ds(start, rows), j * 128 : (j + 1) * 128]
    for j in range(mixed.shape[0]):
        to = slice(j * 128, (j + 1) * 128)
        high[:, to], low[:, to] = parts(mixed[j])


def ket(turns, tensor, rows, lanes, scalars, row_at, count, lane_at, blocks, after):
    states = tensor.shape[1]
    if lanes % 128 or rows % 8 or count * rows % 128:
        flat = [lax.dynamic_slice_in_dim(tensor, scalars[row_at + q] * rows, rows, 0) for q in range(count)]
        flat = jnp.concatenate(flat, 0)
        starts = [scalars[lane_at + j] * lanes + scalars[0] * rows for j in range(blocks)]
        flat = jnp.concatenate([lax.dynamic_slice_in_dim(flat, b, rows, 2) for b in starts], 2)
        return parts_outside(jnp.transpose(flat, (2, 1, 0)).reshape(-1, flat.shape[0]))

    def spec(q):
        return pl.BlockSpec((rows, states, lanes), lambda j, at: (at[row_at + q], 0, at[lane_at + j]))

    block = (rows * states, count * rows)
    out = (pl.BlockSpec(block, lambda j, _: (j, 0)), like((blocks * block[0], block[1]), BF16))
    return turns.call(
        ket_kernel,
        "ket",
        (blocks,),
        [spec(q) for q in range(count)],
        [out] * 2,
        [in_hbm(tensor)] * count,
        scalars,
        [pltpu.VMEM((lanes, count * rows), F32), pltpu.VMEM((count * rows // 128, rows * states, 128), F32)],
        after=after,
        about_us=2.7,
    )


def first_kernel(raw, *refs):
    n = len(raw)
    envs, (sh, sl, op, yh, yl, held) = refs[:n], refs[n:]
    width, _, wide = held.shape
    states = yh.shape[0]
    span = op.shape[1] // width // 2
    at_once = max(1, 512 // wide)

    here = envs[0].shape[0]
    halves = width // here
    step = pl.program_id(0)

    @pl.when(step < halves)
    def _():
        for start in range(0, here, at_once):
            ws = range(start, min(here, start + at_once))
            pick = lambda w: [env[:, w, :] if r else env[w] for r, env in zip(raw, envs)]
            sides = [jnp.concatenate(pick(w), 0) for w in ws]
            eh, el = parts(jnp.concatenate(sides, 1))
            both = stacked_parts(dot_parts(sh[...], sl[...], eh, el), span)
            for j, w in enumerate(ws):
                held[step * here + w] = both[:, j * wide : (j + 1) * wide]

    @pl.when(step >= halves)
    def _():
        groups = yh.shape[1] * states // (op.shape[0] // 2)
        base = (step - halves) * groups
        for start in range(0, groups, at_once):
            gs = range(start, min(groups, start + at_once))
            sides = []
            for g in gs:
                at = pl.ds(pl.multiple_of((base + g) * 2 * span, 2 * span), 2 * span)
                sides.append(jnp.concatenate([held[w, at, :] for w in range(width)], 0))
            out = dot(op[...], jnp.concatenate(sides, 1))
            half = out.shape[0] // 2
            h, l = parts(out[:half] + out[half:])
            size = half // states
            for j, g in enumerate(gs):
                for t in range(states):
                    to = slice(g * size, (g + 1) * size)
                    yh[t, to] = h[t * size : (t + 1) * size, j * wide : (j + 1) * wide]
                    yl[t, to] = l[t * size : (t + 1) * size, j * wide : (j + 1) * wide]


def first_part(turns, own, near, far, start, ket, op, states, b_at, b_count, stays):
    width, rows, wide = own.shape
    made, depth = b_count * states, ket[0].shape[1]
    steps = 4
    shape = (states, made // states * width, wide)
    out = like(shape, BF16) if stays else pltpu.HBM(shape, BF16)
    halves = 2 if width % 16 == 0 else 1
    here = width // halves
    spec = pl.BlockSpec((states, out.shape[1] // steps, wide), lambda i: (0, jnp.maximum(i - halves, 0), 0))
    near_spec = pl.BlockSpec((rows, here, wide), lambda i: (0, jnp.minimum(i, halves - 1), start // wide))
    far_spec = pl.BlockSpec((here, rows, wide), lambda i: (jnp.minimum(i, halves - 1), 0, 0))
    ket_spec = pl.BlockSpec((made, depth), lambda i: (b_at // b_count, 0))
    h, l = turns.call(
        functools.partial(first_kernel, (False, *(True for _ in near), *(False for _ in far))),
        "first_part",
        (halves + steps,),
        [far_spec] + [near_spec] * len(near) + [far_spec] * len(far) + [ket_spec] * 2 + [whole(op)],
        [(spec, out)] * 2,
        [own, *near, *far, *ket, op],
        scratch=[pltpu.VMEM((width, 2 * made, wide), BF16)],
        about_us=3 + 0.03 * wide,
    )
    return (h, l, b_at) if stays else (in_hbm(h), in_hbm(l), b_at)


def second_kernel(n, *refs):
    yhs, yls, (sh, sl), more, out = refs[:n], refs[n : 2 * n], refs[2 * n : 2 * n + 2], refs[2 * n + 2 : -1], refs[-1]
    row = lambda ys: jnp.concatenate([y[t] for t in range(ys[0].shape[0]) for y in ys], 1)
    flat = lambda s: s[...].reshape(-1, s.shape[2])
    total = dot_parts(row(yhs), row(yls), flat(sh), flat(sl)).reshape(out.shape)
    for x in more:
        total += x[...]
    out[...] = total


def second_part(turns, pieces, bra, start, count, width, more, only=None):
    states, depth, columns = bra[0].shape
    pieces = [p for p in pieces if p[2] <= start < p[2] + p[0].shape[1] // width]
    if only is not None:
        pieces = pieces[only : only + 1]
        depth = pieces[0][0].shape[2]
    bra_spec = pl.BlockSpec((states, depth, columns), lambda i: (0, only or 0, 0))
    yhs = [h for h, _, _ in pieces]
    yls = [l for _, l, _ in pieces]
    block = next(b for b in range(min(count, 24), 0, -1) if start % b == 0 and count % b == 0)

    def y_spec(y, base):
        return pl.BlockSpec((states, block * width, y.shape[2]), lambda i: (0, (start - base) // block + i, 0))

    spec = pl.BlockSpec((block, width, columns), lambda i: (i, 0, 0))
    return turns.call(
        functools.partial(second_kernel, len(pieces)),
        "second_part",
        (count // block,),
        [y_spec(y, base) for y, (_, _, base) in zip((*yhs, *yls), pieces * 2)] + [bra_spec] * 2 + [spec] * len(more),
        [(spec, like((count, width, columns), F32))],
        [*yhs, *yls, *bra, *more],
        about_us=3e-2,
    )[0]


def place_kernel(edge, start, old, at, piece, env, *refs):
    out, held, arrived = refs[old], refs[old + 1], refs[old + 2]
    rows = pl.ds(start, piece.shape[0])

    def through(source, target):
        copy = pltpu.make_async_copy(source, target, arrived)
        copy.start()
        copy.wait()

    @pl.when(at[1] == edge)
    def _():
        through(env.at[rows], held)

    @pl.when(at[1] != edge)
    def _():
        through(piece, held)

    through(held, out.at[rows])


def place(turns, piece, env, start, old, scalars, edge):
    spec = pl.BlockSpec(memory_space=pl.ANY)
    return turns.call(
        functools.partial(place_kernel, edge, start, len(old)),
        "place",
        (1,),
        [spec] * (2 + len(old)),
        [(spec, pltpu.HBM(env.shape, F32))],
        [piece, env, *map(in_hbm, old)],
        scalars,
        [pltpu.VMEM(piece.shape, F32), pltpu.SemaphoreType.DMA(())],
        aliases={2 + i: i for i in range(len(old))},
        about_us=1e-1,
    )


def local(sizes, left_env, right_env, left_site, right_site, left_mpo, right_mpo):
    outer, inner, pair = sizes
    n = outer * inner * pair
    chain = lax.axis_size("site")
    index = lambda o, i, p: (o % outer * inner + i % inner) * pair + p % pair

    def moved(x, o=0, i=0, p=0):
        route = []
        for d in range(n):
            do, di, dp = d // (inner * pair), d // pair % inner, d % pair
            route.append((d, index(do + o, di + i, dp + p)))
        return lax.ppermute(x, "bond", route)

    def handed(x, distance):
        return lax.ppermute(x, "site", [(k, k + distance) for k in range(chain) if 0 <= k + distance < chain])

    table = []
    for k in range(chain):
        for d in range(n):
            o, i, p = d // (inner * pair), d // pair % inner, d % pair
            left_rows = [index(o, i - k, p - q) for k in range(inner) for q in range(pair)]
            left_lanes = [index(o + k, i, 0) // pair for k in (*range(1, outer), 0)]
            right_rows = [index(o - k, i, p - q) for k in range(outer) for q in range(pair)]
            right_lanes = [index(o, i + k, 0) // pair for k in (*range(1, inner), 0)]
            table.append([p, k, *left_rows, *left_lanes, *right_rows, *right_lanes])
    scalars = jnp.asarray(table, jnp.int32)[lax.axis_index(("site", "bond"))]

    rows, width, depth = left_env.shape[1:]
    states = left_site.shape[2]
    group = max(1, 128 // (states * width))
    dims = (states, width, width, states, group)
    lane = 128 if depth % 128 == 0 else depth
    cuts = shares(depth, (1, 1), lane)

    class Side:
        def __init__(self, env, tensor, op, gather, reduce, row_at, distance):
            self.env, self.tensor, self.op = in_hbm(env[0]), tensor[0], op
            self.gather, self.reduce, self.row_at, self.distance = gather, reduce, row_at, distance
            self.ranks = {"o": outer, "i": inner}[gather]
            self.others = {"o": outer, "i": inner}[reduce]
            self.pieces = shares(rows, (1, 1) if distance > 0 else (2, 3, 3), group)
            self.own, self.done, self.sent, self.handed, self.out = [], [], [], [], []

        def gather_near(self):
            self.near = [moved(self.env, p=p) for p in range(1, pair)]

        def gather_far(self, x):
            return [moved(x, **{self.gather: k}) for k in range(1, self.ranks)]

        def share(self, far):
            return [y for x in far for y in [x] + [moved(x, p=p) for p in range(1, pair)]]

        def prepare(self, after):
            count = self.ranks * pair
            self.operator = block_operator(turns, self.op, dims)
            self.ket = ket(
                turns, self.tensor, rows, pair * rows, scalars, self.row_at, count, self.row_at + count, self.others, after
            )

        def prepare_bra(self, after):
            self.bra = bra(turns, self.tensor, after)

        def first(self, j, far, b_at, b_count):
            args = self.own[j], self.near, far, sum(cuts[:j]), self.ket, self.operator, states
            self.done.append(first_part(turns, *args, b_at, b_count, j > 0 or self.distance < 0))

        def begin(self):
            starts = [(k - 1) * rows for k in range(1, self.others)]
            args = self.done, self.bra
            self.begun = [second_part(turns, *args, at, self.pieces[0], width, [], 0) for at in starts]

        def send(self, j):
            got = []
            for k in range(1, self.others):
                start = (k - 1) * rows + sum(self.pieces[:j])
                more, only = ([], None) if j else ([self.begun[k - 1]], 1)
                x = second_part(turns, self.done, self.bra, start, self.pieces[j], width, more, only)
                got.append(moved(x, **{self.reduce: k}))
            self.sent.append(got)

        def keep(self, j):
            start = (self.others - 1) * rows + sum(self.pieces[:j])
            x = second_part(turns, self.done, self.bra, start, self.pieces[j], width, self.sent[j])
            self.handed.append(handed(x, self.distance))

        def place(self, j):
            edge = 0 if self.distance > 0 else chain - 1
            self.out = place(turns, self.handed[j], self.env, sum(self.pieces[:j]), self.out, scalars, edge)

    turns = Turns()
    left_op = jnp.transpose(left_mpo[0], (3, 1, 0, 2)).reshape(states * width, -1)
    right_op = jnp.transpose(right_mpo[0], (3, 0, 1, 2)).reshape(states * width, -1)
    left = Side(left_env, left_site, left_op, "i", "o", 2, 1)
    right = Side(right_env, right_site, right_op, "o", "i", 2 + inner * pair + outer, -1)
    both = (left, right)

    far = {}

    def gather(j):
        chunks = cut_columns(turns, [side.env for side in both], sum(cuts[:j]), cuts[j])
        for side, x in zip(both, chunks):
            side.own.append(x)
            far[side, j] = side.gather_far(x)

    def share(j, side):
        far[side, j] = side.share(turns.take(*far[side, j]))

    def first(side, j):
        side.first(j, far[side, j], 0, side.others * rows)

    for side in both:
        side.gather_near()
    gather(0)
    left.prepare(left.near + right.near)
    right.prepare([])
    gather(1)
    for side in both:
        side.prepare_bra([])
    share(0, left)
    share(0, right)
    first(left, 0)
    first(right, 0)
    share(1, left)
    left.begin()
    share(1, right)
    right.begin()
    first(left, 1)
    left.send(0)
    first(right, 1)
    right.send(0)
    left.send(1)
    right.send(1)
    left.keep(0)
    right.keep(0)
    right.send(2)
    right.keep(1)
    left.keep(1)
    left.place(0)
    right.place(0)
    right.keep(2)
    right.place(1)
    left.place(1)
    right.place(2)
    return (left.out[0][None], right.out[0][None])


def solution(mesh):
    return jax.shard_map(
        functools.partial(local, factors(mesh.shape["bond"])),
        mesh=mesh,
        in_specs=(
            P("site", "bond", None, None),
            P("site", "bond", None, None),
            P("site", None, None, None),
            P("site", None, None, None),
            P("site", None, None, None, None),
            P("site", None, None, None, None),
        ),
        out_specs=(P("site", "bond", None, None), P("site", "bond", None, None)),
        check_vma=False,
    )
```

```python
import functools

import jax
import jax.numpy as jnp
from jax import lax
from jax.experimental import pallas as pl
from jax.experimental.pallas import tpu as pltpu
from jax.sharding import PartitionSpec as P

F32 = jnp.float32
BF16 = jnp.bfloat16
VMEM_BYTES = 20 << 20
FLOPS_A_US = 10**11


def factors(n):
    pair = 2 if n % 2 == 0 else 1
    rest = n // pair
    inner = max(d for d in range(1, rest + 1) if rest % d == 0 and d * d <= rest)
    return rest // inner, inner, pair


def shares(total, weights, unit):
    cuts, done, seen = [], 0, 0
    for weight in weights:
        seen += weight
        upto = (total * seen // sum(weights)) // unit * unit
        cuts.append(upto - done)
        done = upto
    cuts[-1] += total - done
    return [c for c in cuts if c]


def parts(x):
    high = x.astype(BF16)
    return high, (x - high.astype(F32)).astype(BF16)


def parts_outside(x):
    high = lax.reduce_precision(x, 8, 7)
    return high.astype(BF16), (x - high).astype(BF16)


def stacked_parts(x, span):
    rows, columns = x.shape
    high = x.astype(BF16).astype(F32)
    both = [y.reshape(rows // span, span, columns) for y in (high, x - high)]
    return jnp.concatenate(both, 1).reshape(2 * rows, columns).astype(BF16)


def dot(a, b):
    return jnp.dot(a, b, preferred_element_type=F32)


def dot_parts(ah, al, bh, bl):
    return dot(ah, bh) + (dot(ah, bl) + dot(al, bh))


def nothing(*_):
    pass


class Turns:
    def __init__(self):
        self.token = None

    def call(self, body, name, grid, ins, outs, operands, scalars=None, scratch=(), aliases=None, about_us=0.3, after=()):
        lead = 0 if scalars is None else 1
        waits = [] if self.token is None else [self.token]
        tokens = len(waits)
        waits += after
        token = like((8, 128), F32)
        skip = lead + len(waits)
        count = len(operands) + len(outs)

        def inner(*refs):
            refs[skip + count][...] = jnp.zeros((8, 128), F32)
            body(*refs[:lead], *refs[skip : skip + count], *refs[skip + count + 1 :])

        *results, self.token = pl.pallas_call(
            inner,
            name=name,
            grid_spec=pltpu.PrefetchScalarGridSpec(
                num_scalar_prefetch=lead,
                grid=grid,
                in_specs=[whole(x) for x in waits[:tokens]] + [pl.BlockSpec(memory_space=pl.ANY)] * len(after) + list(ins),
                out_specs=[x for x, _ in outs] + [whole(token)],
                scratch_shapes=list(scratch),
            ),
            out_shape=[x for _, x in outs] + [token],
            input_output_aliases={skip + i: o for i, o in (aliases or {}).items()},
            compiler_params=pltpu.CompilerParams(vmem_limit_bytes=VMEM_BYTES),
            cost_estimate=pl.CostEstimate(flops=int(about_us * FLOPS_A_US), bytes_accessed=1000, transcendentals=0),
        )(*([] if scalars is None else [scalars]), *waits, *operands)
        return results


    def take(self, *arrays):
        spec = pl.BlockSpec(memory_space=pl.ANY)
        outs = [(spec, pltpu.HBM(x.shape, x.dtype)) for x in arrays]
        same = {i: i for i in range(len(arrays))}
        return self.call(nothing, "take", (1,), [spec] * len(arrays), outs, [in_hbm(x) for x in arrays], aliases=same)


def whole(x):
    zeros = (0,) * len(x.shape)
    return pl.BlockSpec(tuple(x.shape), lambda *_: zeros)


def like(shape, dtype):
    return jax.ShapeDtypeStruct(tuple(shape), dtype)


def in_hbm(x):
    return pltpu.with_memory_space_constraint(x, pltpu.HBM)


def ids(dims, axis):
    return lax.broadcasted_iota(jnp.int32, dims, axis)


def cut_kernel(*refs):
    half = len(refs) // 2
    for x, out in zip(refs[:half], refs[half:]):
        for w in range(out.shape[0]):
            out[w] = x[:, w, :]


def cut_columns(turns, envs, start, wide):
    rows, width, _ = envs[0].shape
    spec = pl.BlockSpec((rows, width, wide), lambda i: (0, 0, start // wide))
    out = like((width, rows, wide), F32)
    return turns.call(cut_kernel, "cut_columns", (1,), [spec] * len(envs), [(whole(out), out)] * len(envs), envs)


def operator_kernel(dims, op, out):
    t, v, w, s, g = dims
    rows, columns = t * g * v, w * 2 * g * s
    row, at = ids((rows, t * v), 0), ids((rows, t * v), 1)
    spread = (row // (g * v) * v + row % v == at).astype(F32).astype(BF16)
    at, column = ids((w * s, columns), 0), ids((w * s, columns), 1)
    along = (column // (2 * g * s) * s + column % s == at).astype(F32).astype(BF16)
    row, column = ids((rows, columns), 0), ids((rows, columns), 1)
    same = row // v % g == column // s % g
    low_rows = column // (g * s) % 2 == 1
    high, low = (dot(dot(spread, part).astype(BF16), along) for part in parts(op[...]))
    out[:rows] = jnp.where(same, high, 0.0).astype(BF16)
    out[rows:] = jnp.where(same, jnp.where(low_rows, 0.0, low), 0.0).astype(BF16)


def block_operator(turns, op, dims):
    t, v, w, s, g = dims
    out = like((2 * t * g * v, 2 * w * g * s), BF16)
    return turns.call(
        functools.partial(operator_kernel, dims), "operator", (1,), [whole(op)], [(whole(out), out)], [op]
    )[0]


def bra_kernel(tensor, high, low):
    step, states, _ = tensor.shape
    span = min(step, 32)
    row, at = ids((span * states, span * states), 0), ids((span * states, span * states), 1)
    order = (row % span * states + row // span == at).astype(F32).astype(BF16)
    for start in range(0, step, span):
        x = tensor[start : start + span].reshape(span * states, -1)
        for part, out in zip(parts(x), (high, low)):
            y = dot(order, part).astype(BF16)
            for t in range(states):
                out[t, start : start + span] = y[t * span : (t + 1) * span]


def bra(turns, tensor, after):
    depth, states, wide = tensor.shape
    step = min(depth, 128)
    out = like((states, depth, wide), BF16)
    spec = pl.BlockSpec((states, step, wide), lambda i: (0, i, 0))
    return turns.call(
        bra_kernel,
        "bra",
        (depth // step,),
        [pl.BlockSpec((step, states, wide), lambda i: (i, 0, 0))],
        [(spec, out)] * 2,
        [tensor],
        after=after,
        about_us=4,
    )


def ket_kernel(at, *refs):
    tensors, (high, low, turned, mixed) = refs[:-4], refs[-4:]
    rows, states, _ = tensors[0].shape
    start = pl.multiple_of(at[0] * rows, rows)
    for s in range(states):
        turned[...] = jnp.concatenate([tensor[:, s, :] for tensor in tensors], 0).T
        for j in range(mixed.shape[0]):
            mixed[j, pl.ds(s, rows, stride=states), :] = turned[pl.ds(start, rows), j * 128 : (j + 1) * 128]
    for j in range(mixed.shape[0]):
        to = slice(j * 128, (j + 1) * 128)
        high[:, to], low[:, to] = parts(mixed[j])


def ket(turns, tensor, rows, lanes, scalars, row_at, count, lane_at, blocks, after):
    states = tensor.shape[1]
    if lanes % 128 or rows % 8 or count * rows % 128:
        flat = [lax.dynamic_slice_in_dim(tensor, scalars[row_at + q] * rows, rows, 0) for q in range(count)]
        flat = jnp.concatenate(flat, 0)
        starts = [scalars[lane_at + j] * lanes + scalars[0] * rows for j in range(blocks)]
        flat = jnp.concatenate([lax.dynamic_slice_in_dim(flat, b, rows, 2) for b in starts], 2)
        return parts_outside(jnp.transpose(flat, (2, 1, 0)).reshape(-1, flat.shape[0]))

    def spec(q):
        return pl.BlockSpec((rows, states, lanes), lambda j, at: (at[row_at + q], 0, at[lane_at + j]))

    block = (rows * states, count * rows)
    out = (pl.BlockSpec(block, lambda j, _: (j, 0)), like((blocks * block[0], block[1]), BF16))
    return turns.call(
        ket_kernel,
        "ket",
        (blocks,),
        [spec(q) for q in range(count)],
        [out] * 2,
        [in_hbm(tensor)] * count,
        scalars,
        [pltpu.VMEM((lanes, count * rows), F32), pltpu.VMEM((count * rows // 128, rows * states, 128), F32)],
        after=after,
        about_us=2.7,
    )


def first_kernel(raw, *refs):
    n = len(raw)
    envs, (sh, sl, op, yh, yl, held) = refs[:n], refs[n:]
    width, _, wide = held.shape
    states = yh.shape[0]
    span = op.shape[1] // width // 2
    at_once = max(1, 512 // wide)

    here = envs[0].shape[0]
    halves = width // here
    step = pl.program_id(0)

    @pl.when(step < halves)
    def _():
        for start in range(0, here, at_once):
            ws = range(start, min(here, start + at_once))
            pick = lambda w: [env[:, w, :] if r else env[w] for r, env in zip(raw, envs)]
            sides = [jnp.concatenate(pick(w), 0) for w in ws]
            eh, el = parts(jnp.concatenate(sides, 1))
            both = stacked_parts(dot_parts(sh[...], sl[...], eh, el), span)
            for j, w in enumerate(ws):
                held[step * here + w] = both[:, j * wide : (j + 1) * wide]

    @pl.when(step >= halves)
    def _():
        groups = yh.shape[1] * states // (op.shape[0] // 2)
        base = (step - halves) * groups
        for start in range(0, groups, at_once):
            gs = range(start, min(groups, start + at_once))
            sides = []
            for g in gs:
                at = pl.ds(pl.multiple_of((base + g) * 2 * span, 2 * span), 2 * span)
                sides.append(jnp.concatenate([held[w, at, :] for w in range(width)], 0))
            out = dot(op[...], jnp.concatenate(sides, 1))
            half = out.shape[0] // 2
            h, l = parts(out[:half] + out[half:])
            size = half // states
            for j, g in enumerate(gs):
                for t in range(states):
                    to = slice(g * size, (g + 1) * size)
                    yh[t, to] = h[t * size : (t + 1) * size, j * wide : (j + 1) * wide]
                    yl[t, to] = l[t * size : (t + 1) * size, j * wide : (j + 1) * wide]


def first_part(turns, own, near, far, start, ket, op, states, b_at, b_count, stays):
    width, rows, wide = own.shape
    made, depth = b_count * states, ket[0].shape[1]
    steps = 4
    shape = (states, made // states * width, wide)
    out = like(shape, BF16) if stays else pltpu.HBM(shape, BF16)
    halves = 2 if width % 16 == 0 else 1
    here = width // halves
    spec = pl.BlockSpec((states, out.shape[1] // steps, wide), lambda i: (0, jnp.maximum(i - halves, 0), 0))
    near_spec = pl.BlockSpec((rows, here, wide), lambda i: (0, jnp.minimum(i, halves - 1), start // wide))
    far_spec = pl.BlockSpec((here, rows, wide), lambda i: (jnp.minimum(i, halves - 1), 0, 0))
    ket_spec = pl.BlockSpec((made, depth), lambda i: (b_at // b_count, 0))
    h, l = turns.call(
        functools.partial(first_kernel, (False, *(True for _ in near), *(False for _ in far))),
        "first_part",
        (halves + steps,),
        [far_spec] + [near_spec] * len(near) + [far_spec] * len(far) + [ket_spec] * 2 + [whole(op)],
        [(spec, out)] * 2,
        [own, *near, *far, *ket, op],
        scratch=[pltpu.VMEM((width, 2 * made, wide), BF16)],
        about_us=3 + 0.03 * wide,
    )
    return (h, l, b_at) if stays else (in_hbm(h), in_hbm(l), b_at)


def second_kernel(n, *refs):
    yhs, yls, (sh, sl), more, out = refs[:n], refs[n : 2 * n], refs[2 * n : 2 * n + 2], refs[2 * n + 2 : -1], refs[-1]
    row = lambda ys: jnp.concatenate([y[t] for t in range(ys[0].shape[0]) for y in ys], 1)
    flat = lambda s: s[...].reshape(-1, s.shape[2])
    total = dot_parts(row(yhs), row(yls), flat(sh), flat(sl)).reshape(out.shape)
    for x in more:
        total += x[...]
    out[...] = total


def second_part(turns, pieces, bra, start, count, width, more, only=None):
    states, depth, columns = bra[0].shape
    pieces = [p for p in pieces if p[2] <= start < p[2] + p[0].shape[1] // width]
    if only is not None:
        pieces = pieces[only : only + 1]
        depth = pieces[0][0].shape[2]
    bra_spec = pl.BlockSpec((states, depth, columns), lambda i: (0, only or 0, 0))
    yhs = [h for h, _, _ in pieces]
    yls = [l for _, l, _ in pieces]
    block = next(b for b in range(min(count, 24), 0, -1) if start % b == 0 and count % b == 0)

    def y_spec(y, base):
        return pl.BlockSpec((states, block * width, y.shape[2]), lambda i: (0, (start - base) // block + i, 0))

    spec = pl.BlockSpec((block, width, columns), lambda i: (i, 0, 0))
    return turns.call(
        functools.partial(second_kernel, len(pieces)),
        "second_part",
        (count // block,),
        [y_spec(y, base) for y, (_, _, base) in zip((*yhs, *yls), pieces * 2)] + [bra_spec] * 2 + [spec] * len(more),
        [(spec, like((count, width, columns), F32))],
        [*yhs, *yls, *bra, *more],
        about_us=3e-2,
    )[0]


def place_kernel(edge, start, old, at, piece, env, *refs):
    out, held, arrived = refs[old], refs[old + 1], refs[old + 2]
    rows = pl.ds(start, piece.shape[0])

    def through(source, target):
        copy = pltpu.make_async_copy(source, target, arrived)
        copy.start()
        copy.wait()

    @pl.when(at[1] == edge)
    def _():
        through(env.at[rows], held)

    @pl.when(at[1] != edge)
    def _():
        through(piece, held)

    through(held, out.at[rows])


def place(turns, piece, env, start, old, scalars, edge):
    spec = pl.BlockSpec(memory_space=pl.ANY)
    return turns.call(
        functools.partial(place_kernel, edge, start, len(old)),
        "place",
        (1,),
        [spec] * (2 + len(old)),
        [(spec, pltpu.HBM(env.shape, F32))],
        [piece, env, *map(in_hbm, old)],
        scalars,
        [pltpu.VMEM(piece.shape, F32), pltpu.SemaphoreType.DMA(())],
        aliases={2 + i: i for i in range(len(old))},
        about_us=1e-1,
    )


def local(sizes, left_env, right_env, left_site, right_site, left_mpo, right_mpo):
    outer, inner, pair = sizes
    n = outer * inner * pair
    chain = lax.axis_size("site")
    index = lambda o, i, p: (o % outer * inner + i % inner) * pair + p % pair

    def moved(x, o=0, i=0, p=0):
        route = []
        for d in range(n):
            do, di, dp = d // (inner * pair), d // pair % inner, d % pair
            route.append((d, index(do + o, di + i, dp + p)))
        return lax.ppermute(x, "bond", route)

    def handed(x, distance):
        return lax.ppermute(x, "site", [(k, k + distance) for k in range(chain) if 0 <= k + distance < chain])

    table = []
    for k in range(chain):
        for d in range(n):
            o, i, p = d // (inner * pair), d // pair % inner, d % pair
            left_rows = [index(o, i - k, p - q) for k in range(inner) for q in range(pair)]
            left_lanes = [index(o + k, i, 0) // pair for k in (*range(1, outer), 0)]
            right_rows = [index(o - k, i, p - q) for k in range(outer) for q in range(pair)]
            right_lanes = [index(o, i + k, 0) // pair for k in (*range(1, inner), 0)]
            table.append([p, k, *left_rows, *left_lanes, *right_rows, *right_lanes])
    scalars = jnp.asarray(table, jnp.int32)[lax.axis_index(("site", "bond"))]

    rows, width, depth = left_env.shape[1:]
    states = left_site.shape[2]
    group = max(1, 128 // (states * width))
    dims = (states, width, width, states, group)
    lane = 128 if depth % 128 == 0 else depth
    cuts = shares(depth, (1, 1), lane)

    class Side:
        def __init__(self, env, tensor, op, gather, reduce, row_at, distance):
            self.env, self.tensor, self.op = in_hbm(env[0]), tensor[0], op
            self.gather, self.reduce, self.row_at, self.distance = gather, reduce, row_at, distance
            self.ranks = {"o": outer, "i": inner}[gather]
            self.others = {"o": outer, "i": inner}[reduce]
            self.pieces = shares(rows, (1, 1) if distance > 0 else (2, 3, 3), group)
            self.own, self.done, self.sent, self.handed, self.out = [], [], [], [], []

        def gather_near(self):
            self.near = [moved(self.env, p=p) for p in range(1, pair)]

        def gather_far(self, x):
            return [moved(x, **{self.gather: k}) for k in range(1, self.ranks)]

        def share(self, far):
            return [y for x in far for y in [x] + [moved(x, p=p) for p in range(1, pair)]]

        def prepare(self, after):
            count = self.ranks * pair
            self.operator = block_operator(turns, self.op, dims)
            self.ket = ket(
                turns, self.tensor, rows, pair * rows, scalars, self.row_at, count, self.row_at + count, self.others, after
            )

        def prepare_bra(self, after):
            self.bra = bra(turns, self.tensor, after)

        def first(self, j, far, b_at, b_count):
            args = self.own[j], self.near, far, sum(cuts[:j]), self.ket, self.operator, states
            self.done.append(first_part(turns, *args, b_at, b_count, j > 0 or self.distance < 0))

        def begin(self):
            starts = [(k - 1) * rows for k in range(1, self.others)]
            args = self.done, self.bra
            self.begun = [second_part(turns, *args, at, self.pieces[0], width, [], 0) for at in starts]

        def send(self, j):
            got = []
            for k in range(1, self.others):
                start = (k - 1) * rows + sum(self.pieces[:j])
                more, only = ([], None) if j else ([self.begun[k - 1]], 1)
                x = second_part(turns, self.done, self.bra, start, self.pieces[j], width, more, only)
                got.append(moved(x, **{self.reduce: k}))
            self.sent.append(got)

        def keep(self, j):
            start = (self.others - 1) * rows + sum(self.pieces[:j])
            x = second_part(turns, self.done, self.bra, start, self.pieces[j], width, self.sent[j])
            self.handed.append(handed(x, self.distance))

        def place(self, j):
            edge = 0 if self.distance > 0 else chain - 1
            self.out = place(turns, self.handed[j], self.env, sum(self.pieces[:j]), self.out, scalars, edge)

    turns = Turns()
    left_op = jnp.transpose(left_mpo[0], (3, 1, 0, 2)).reshape(states * width, -1)
    right_op = jnp.transpose(right_mpo[0], (3, 0, 1, 2)).reshape(states * width, -1)
    left = Side(left_env, left_site, left_op, "i", "o", 2, 1)
    right = Side(right_env, right_site, right_op, "o", "i", 2 + inner * pair + outer, -1)
    both = (left, right)

    far = {}

    def gather(j):
        chunks = cut_columns(turns, [side.env for side in both], sum(cuts[:j]), cuts[j])
        for side, x in zip(both, chunks):
            side.own.append(x)
            far[side, j] = side.gather_far(x)

    def share(j, side):
        far[side, j] = side.share(turns.take(*far[side, j]))

    def first(side, j):
        side.first(j, far[side, j], 0, side.others * rows)

    for side in both:
        side.gather_near()
    gather(0)
    left.prepare(left.near + right.near)
    right.prepare([])
    gather(1)
    for side in both:
        side.prepare_bra([])
    share(0, left)
    share(0, right)
    first(left, 0)
    first(right, 0)
    share(1, left)
    left.begin()
    share(1, right)
    right.begin()
    first(left, 1)
    left.send(0)
    first(right, 1)
    right.send(0)
    left.send(1)
    right.send(1)
    left.keep(0)
    right.keep(0)
    right.send(2)
    right.keep(1)
    left.keep(1)
    left.place(0)
    right.place(0)
    right.keep(2)
    right.place(1)
    left.place(1)
    right.place(2)
    return (left.out[0][None], right.out[0][None])


def solution(mesh):
    return jax.shard_map(
        functools.partial(local, factors(mesh.shape["bond"])),
        mesh=mesh,
        in_specs=(
            P("site", "bond", None, None),
            P("site", "bond", None, None),
            P("site", None, None, None),
            P("site", None, None, None),
            P("site", None, None, None, None),
            P("site", None, None, None, None),
        ),
        out_specs=(P("site", "bond", None, None), P("site", "bond", None, None)),
        check_vma=False,
    )
```

```python
import functools

import jax
import jax.numpy as jnp
from jax import lax
from jax.experimental import pallas as pl
from jax.experimental.pallas import tpu as pltpu
from jax.sharding import PartitionSpec as P

F32 = jnp.float32
BF16 = jnp.bfloat16
VMEM_BYTES = 20 << 20
FLOPS_A_US = 10**11


def factors(n):
    pair = 2 if n % 2 == 0 else 1
    rest = n // pair
    inner = max(d for d in range(1, rest + 1) if rest % d == 0 and d * d <= rest)
    return rest // inner, inner, pair


def shares(total, weights, unit):
    cuts, done, seen = [], 0, 0
    for weight in weights:
        seen += weight
        upto = (total * seen // sum(weights)) // unit * unit
        cuts.append(upto - done)
        done = upto
    cuts[-1] += total - done
    return [c for c in cuts if c]


def parts(x):
    high = x.astype(BF16)
    return high, (x - high.astype(F32)).astype(BF16)


def parts_outside(x):
    high = lax.reduce_precision(x, 8, 7)
    return high.astype(BF16), (x - high).astype(BF16)


def stacked_parts(x, span):
    rows, columns = x.shape
    high = x.astype(BF16).astype(F32)
    both = [y.reshape(rows // span, span, columns) for y in (high, x - high)]
    return jnp.concatenate(both, 1).reshape(2 * rows, columns).astype(BF16)


def dot(a, b):
    return jnp.dot(a, b, preferred_element_type=F32)


def dot_parts(ah, al, bh, bl):
    return dot(ah, bh) + (dot(ah, bl) + dot(al, bh))


def nothing(*_):
    pass


class Turns:
    def __init__(self):
        self.token = None

    def call(self, body, name, grid, ins, outs, operands, scalars=None, scratch=(), aliases=None, about_us=0.3, after=()):
        lead = 0 if scalars is None else 1
        waits = [] if self.token is None else [self.token]
        tokens = len(waits)
        waits += after
        token = like((8, 128), F32)
        skip = lead + len(waits)
        count = len(operands) + len(outs)

        def inner(*refs):
            refs[skip + count][...] = jnp.zeros((8, 128), F32)
            body(*refs[:lead], *refs[skip : skip + count], *refs[skip + count + 1 :])

        *results, self.token = pl.pallas_call(
            inner,
            name=name,
            grid_spec=pltpu.PrefetchScalarGridSpec(
                num_scalar_prefetch=lead,
                grid=grid,
                in_specs=[whole(x) for x in waits[:tokens]] + [pl.BlockSpec(memory_space=pl.ANY)] * len(after) + list(ins),
                out_specs=[x for x, _ in outs] + [whole(token)],
                scratch_shapes=list(scratch),
            ),
            out_shape=[x for _, x in outs] + [token],
            input_output_aliases={skip + i: o for i, o in (aliases or {}).items()},
            compiler_params=pltpu.CompilerParams(vmem_limit_bytes=VMEM_BYTES),
            cost_estimate=pl.CostEstimate(flops=int(about_us * FLOPS_A_US), bytes_accessed=1000, transcendentals=0),
        )(*([] if scalars is None else [scalars]), *waits, *operands)
        return results


    def take(self, *arrays):
        spec = pl.BlockSpec(memory_space=pl.ANY)
        outs = [(spec, pltpu.HBM(x.shape, x.dtype)) for x in arrays]
        same = {i: i for i in range(len(arrays))}
        return self.call(nothing, "take", (1,), [spec] * len(arrays), outs, [in_hbm(x) for x in arrays], aliases=same)


def whole(x):
    zeros = (0,) * len(x.shape)
    return pl.BlockSpec(tuple(x.shape), lambda *_: zeros)


def like(shape, dtype):
    return jax.ShapeDtypeStruct(tuple(shape), dtype)


def in_hbm(x):
    return pltpu.with_memory_space_constraint(x, pltpu.HBM)


def ids(dims, axis):
    return lax.broadcasted_iota(jnp.int32, dims, axis)


def cut_kernel(*refs):
    half = len(refs) // 2
    for x, out in zip(refs[:half], refs[half:]):
        for w in range(out.shape[0]):
            out[w] = x[:, w, :]


def cut_columns(turns, envs, start, wide):
    rows, width, _ = envs[0].shape
    spec = pl.BlockSpec((rows, width, wide), lambda i: (0, 0, start // wide))
    out = like((width, rows, wide), F32)
    return turns.call(cut_kernel, "cut_columns", (1,), [spec] * len(envs), [(whole(out), out)] * len(envs), envs)


def operator_kernel(dims, op, out):
    t, v, w, s, g = dims
    rows, columns = t * g * v, w * 2 * g * s
    row, at = ids((rows, t * v), 0), ids((rows, t * v), 1)
    spread = (row // (g * v) * v + row % v == at).astype(F32).astype(BF16)
    at, column = ids((w * s, columns), 0), ids((w * s, columns), 1)
    along = (column // (2 * g * s) * s + column % s == at).astype(F32).astype(BF16)
    row, column = ids((rows, columns), 0), ids((rows, columns), 1)
    same = row // v % g == column // s % g
    low_rows = column // (g * s) % 2 == 1
    high, low = (dot(dot(spread, part).astype(BF16), along) for part in parts(op[...]))
    out[:rows] = jnp.where(same, high, 0.0).astype(BF16)
    out[rows:] = jnp.where(same, jnp.where(low_rows, 0.0, low), 0.0).astype(BF16)


def block_operator(turns, op, dims):
    t, v, w, s, g = dims
    out = like((2 * t * g * v, 2 * w * g * s), BF16)
    return turns.call(
        functools.partial(operator_kernel, dims), "operator", (1,), [whole(op)], [(whole(out), out)], [op]
    )[0]


def bra_kernel(tensor, high, low):
    step, states, _ = tensor.shape
    span = min(step, 32)
    row, at = ids((span * states, span * states), 0), ids((span * states, span * states), 1)
    order = (row % span * states + row // span == at).astype(F32).astype(BF16)
    for start in range(0, step, span):
        x = tensor[start : start + span].reshape(span * states, -1)
        for part, out in zip(parts(x), (high, low)):
            y = dot(order, part).astype(BF16)
            for t in range(states):
                out[t, start : start + span] = y[t * span : (t + 1) * span]


def bra(turns, tensor, after):
    depth, states, wide = tensor.shape
    step = min(depth, 128)
    out = like((states, depth, wide), BF16)
    spec = pl.BlockSpec((states, step, wide), lambda i: (0, i, 0))
    return turns.call(
        bra_kernel,
        "bra",
        (depth // step,),
        [pl.BlockSpec((step, states, wide), lambda i: (i, 0, 0))],
        [(spec, out)] * 2,
        [tensor],
        after=after,
        about_us=4,
    )


def ket_kernel(at, *refs):
    tensors, (high, low, turned, mixed) = refs[:-4], refs[-4:]
    rows, states, _ = tensors[0].shape
    start = pl.multiple_of(at[0] * rows, rows)
    for s in range(states):
        turned[...] = jnp.concatenate([tensor[:, s, :] for tensor in tensors], 0).T
        for j in range(mixed.shape[0]):
            mixed[j, pl.ds(s, rows, stride=states), :] = turned[pl.ds(start, rows), j * 128 : (j + 1) * 128]
    for j in range(mixed.shape[0]):
        to = slice(j * 128, (j + 1) * 128)
        high[:, to], low[:, to] = parts(mixed[j])


def ket(turns, tensor, rows, lanes, scalars, row_at, count, lane_at, blocks, after):
    states = tensor.shape[1]
    if lanes % 128 or rows % 8 or count * rows % 128:
        flat = [lax.dynamic_slice_in_dim(tensor, scalars[row_at + q] * rows, rows, 0) for q in range(count)]
        flat = jnp.concatenate(flat, 0)
        starts = [scalars[lane_at + j] * lanes + scalars[0] * rows for j in range(blocks)]
        flat = jnp.concatenate([lax.dynamic_slice_in_dim(flat, b, rows, 2) for b in starts], 2)
        return parts_outside(jnp.transpose(flat, (2, 1, 0)).reshape(-1, flat.shape[0]))

    def spec(q):
        return pl.BlockSpec((rows, states, lanes), lambda j, at: (at[row_at + q], 0, at[lane_at + j]))

    block = (rows * states, count * rows)
    out = (pl.BlockSpec(block, lambda j, _: (j, 0)), like((blocks * block[0], block[1]), BF16))
    return turns.call(
        ket_kernel,
        "ket",
        (blocks,),
        [spec(q) for q in range(count)],
        [out] * 2,
        [in_hbm(tensor)] * count,
        scalars,
        [pltpu.VMEM((lanes, count * rows), F32), pltpu.VMEM((count * rows // 128, rows * states, 128), F32)],
        after=after,
        about_us=2.7,
    )


def first_kernel(raw, *refs):
    n = len(raw)
    envs, (sh, sl, op, yh, yl, held) = refs[:n], refs[n:]
    width, _, wide = held.shape
    states = yh.shape[0]
    span = op.shape[1] // width // 2
    at_once = max(1, 512 // wide)

    here = envs[0].shape[0]
    halves = width // here
    step = pl.program_id(0)

    @pl.when(step < halves)
    def _():
        for start in range(0, here, at_once):
            ws = range(start, min(here, start + at_once))
            pick = lambda w: [env[:, w, :] if r else env[w] for r, env in zip(raw, envs)]
            sides = [jnp.concatenate(pick(w), 0) for w in ws]
            eh, el = parts(jnp.concatenate(sides, 1))
            both = stacked_parts(dot_parts(sh[...], sl[...], eh, el), span)
            for j, w in enumerate(ws):
                held[step * here + w] = both[:, j * wide : (j + 1) * wide]

    @pl.when(step >= halves)
    def _():
        groups = yh.shape[1] * states // (op.shape[0] // 2)
        base = (step - halves) * groups
        for start in range(0, groups, at_once):
            gs = range(start, min(groups, start + at_once))
            sides = []
            for g in gs:
                at = pl.ds(pl.multiple_of((base + g) * 2 * span, 2 * span), 2 * span)
                sides.append(jnp.concatenate([held[w, at, :] for w in range(width)], 0))
            out = dot(op[...], jnp.concatenate(sides, 1))
            half = out.shape[0] // 2
            h, l = parts(out[:half] + out[half:])
            size = half // states
            for j, g in enumerate(gs):
                for t in range(states):
                    to = slice(g * size, (g + 1) * size)
                    yh[t, to] = h[t * size : (t + 1) * size, j * wide : (j + 1) * wide]
                    yl[t, to] = l[t * size : (t + 1) * size, j * wide : (j + 1) * wide]


def first_part(turns, own, near, far, start, ket, op, states, b_at, b_count, stays):
    width, rows, wide = own.shape
    made, depth = b_count * states, ket[0].shape[1]
    steps = 4
    shape = (states, made // states * width, wide)
    out = like(shape, BF16) if stays else pltpu.HBM(shape, BF16)
    halves = 2 if width % 16 == 0 else 1
    here = width // halves
    spec = pl.BlockSpec((states, out.shape[1] // steps, wide), lambda i: (0, jnp.maximum(i - halves, 0), 0))
    near_spec = pl.BlockSpec((rows, here, wide), lambda i: (0, jnp.minimum(i, halves - 1), start // wide))
    far_spec = pl.BlockSpec((here, rows, wide), lambda i: (jnp.minimum(i, halves - 1), 0, 0))
    ket_spec = pl.BlockSpec((made, depth), lambda i: (b_at // b_count, 0))
    h, l = turns.call(
        functools.partial(first_kernel, (False, *(True for _ in near), *(False for _ in far))),
        "first_part",
        (halves + steps,),
        [far_spec] + [near_spec] * len(near) + [far_spec] * len(far) + [ket_spec] * 2 + [whole(op)],
        [(spec, out)] * 2,
        [own, *near, *far, *ket, op],
        scratch=[pltpu.VMEM((width, 2 * made, wide), BF16)],
        about_us=3 + 0.03 * wide,
    )
    return (h, l, b_at) if stays else (in_hbm(h), in_hbm(l), b_at)


def second_kernel(n, *refs):
    yhs, yls, (sh, sl), more, out = refs[:n], refs[n : 2 * n], refs[2 * n : 2 * n + 2], refs[2 * n + 2 : -1], refs[-1]
    row = lambda ys: jnp.concatenate([y[t] for t in range(ys[0].shape[0]) for y in ys], 1)
    flat = lambda s: s[...].reshape(-1, s.shape[2])
    total = dot_parts(row(yhs), row(yls), flat(sh), flat(sl)).reshape(out.shape)
    for x in more:
        total += x[...]
    out[...] = total


def second_part(turns, pieces, bra, start, count, width, more, only=None):
    states, depth, columns = bra[0].shape
    pieces = [p for p in pieces if p[2] <= start < p[2] + p[0].shape[1] // width]
    if only is not None:
        pieces = pieces[only : only + 1]
        depth = pieces[0][0].shape[2]
    bra_spec = pl.BlockSpec((states, depth, columns), lambda i: (0, only or 0, 0))
    yhs = [h for h, _, _ in pieces]
    yls = [l for _, l, _ in pieces]
    block = next(b for b in range(min(count, 16), 0, -1) if start % b == 0 and count % b == 0)

    def y_spec(y, base):
        return pl.BlockSpec((states, block * width, y.shape[2]), lambda i: (0, (start - base) // block + i, 0))

    spec = pl.BlockSpec((block, width, columns), lambda i: (i, 0, 0))
    return turns.call(
        functools.partial(second_kernel, len(pieces)),
        "second_part",
        (count // block,),
        [y_spec(y, base) for y, (_, _, base) in zip((*yhs, *yls), pieces * 2)] + [bra_spec] * 2 + [spec] * len(more),
        [(spec, like((count, width, columns), F32))],
        [*yhs, *yls, *bra, *more],
        about_us=3e-2,
    )[0]


def place_kernel(edge, start, old, at, piece, env, *refs):
    out, held, arrived = refs[old], refs[old + 1], refs[old + 2]
    rows = pl.ds(start, piece.shape[0])

    def through(source, target):
        copy = pltpu.make_async_copy(source, target, arrived)
        copy.start()
        copy.wait()

    @pl.when(at[1] == edge)
    def _():
        through(env.at[rows], held)

    @pl.when(at[1] != edge)
    def _():
        through(piece, held)

    through(held, out.at[rows])


def place(turns, piece, env, start, old, scalars, edge):
    spec = pl.BlockSpec(memory_space=pl.ANY)
    return turns.call(
        functools.partial(place_kernel, edge, start, len(old)),
        "place",
        (1,),
        [spec] * (2 + len(old)),
        [(spec, pltpu.HBM(env.shape, F32))],
        [piece, env, *map(in_hbm, old)],
        scalars,
        [pltpu.VMEM(piece.shape, F32), pltpu.SemaphoreType.DMA(())],
        aliases={2 + i: i for i in range(len(old))},
        about_us=1e-1,
    )


def local(sizes, left_env, right_env, left_site, right_site, left_mpo, right_mpo):
    outer, inner, pair = sizes
    n = outer * inner * pair
    chain = lax.axis_size("site")
    index = lambda o, i, p: (o % outer * inner + i % inner) * pair + p % pair

    def moved(x, o=0, i=0, p=0):
        route = []
        for d in range(n):
            do, di, dp = d // (inner * pair), d // pair % inner, d % pair
            route.append((d, index(do + o, di + i, dp + p)))
        return lax.ppermute(x, "bond", route)

    def handed(x, distance):
        return lax.ppermute(x, "site", [(k, k + distance) for k in range(chain) if 0 <= k + distance < chain])

    table = []
    for k in range(chain):
        for d in range(n):
            o, i, p = d // (inner * pair), d // pair % inner, d % pair
            left_rows = [index(o, i - k, p - q) for k in range(inner) for q in range(pair)]
            left_lanes = [index(o + k, i, 0) // pair for k in (*range(1, outer), 0)]
            right_rows = [index(o - k, i, p - q) for k in range(outer) for q in range(pair)]
            right_lanes = [index(o, i + k, 0) // pair for k in (*range(1, inner), 0)]
            table.append([p, k, *left_rows, *left_lanes, *right_rows, *right_lanes])
    scalars = jnp.asarray(table, jnp.int32)[lax.axis_index(("site", "bond"))]

    rows, width, depth = left_env.shape[1:]
    states = left_site.shape[2]
    group = max(1, 128 // (states * width))
    dims = (states, width, width, states, group)
    lane = 128 if depth % 128 == 0 else depth
    cuts = shares(depth, (1, 1), lane)

    class Side:
        def __init__(self, env, tensor, op, gather, reduce, row_at, distance):
            self.env, self.tensor, self.op = in_hbm(env[0]), tensor[0], op
            self.gather, self.reduce, self.row_at, self.distance = gather, reduce, row_at, distance
            self.ranks = {"o": outer, "i": inner}[gather]
            self.others = {"o": outer, "i": inner}[reduce]
            self.pieces = shares(rows, (1, 1) if distance > 0 else (2, 3, 3), group)
            self.starts = [rows - self.pieces[0]] + [sum(self.pieces[1:j]) for j in range(1, len(self.pieces))]
            self.own, self.done, self.sent, self.handed, self.out = [], [], [], [], []

        def gather_near(self):
            self.near = [moved(self.env, p=p) for p in range(1, pair)]

        def gather_far(self, x):
            return [moved(x, **{self.gather: k}) for k in range(1, self.ranks)]

        def share(self, far):
            return [y for x in far for y in [x] + [moved(x, p=p) for p in range(1, pair)]]

        def prepare(self, after):
            count = self.ranks * pair
            self.operator = block_operator(turns, self.op, dims)
            self.ket = ket(
                turns, self.tensor, rows, pair * rows, scalars, self.row_at, count, self.row_at + count, self.others, after
            )

        def prepare_bra(self, after):
            self.bra = bra(turns, self.tensor, after)

        def first(self, j, far, b_at, b_count):
            args = self.own[j], self.near, far, sum(cuts[:j]), self.ket, self.operator, states
            self.done.append(first_part(turns, *args, b_at, b_count, j > 0 or self.distance < 0))

        def begin(self):
            starts = [(k - 1) * rows + self.starts[0] for k in range(1, self.others)]
            args = self.done, self.bra
            self.begun = [second_part(turns, *args, at, self.pieces[0], width, [], 0) for at in starts]

        def send(self, j):
            got = []
            for k in range(1, self.others):
                start = (k - 1) * rows + self.starts[j]
                more, only = ([], None) if j else ([self.begun[k - 1]], 1)
                x = second_part(turns, self.done, self.bra, start, self.pieces[j], width, more, only)
                got.append(moved(x, **{self.reduce: k}))
            self.sent.append(got)

        def keep(self, j):
            start = (self.others - 1) * rows + self.starts[j]
            x = second_part(turns, self.done, self.bra, start, self.pieces[j], width, self.sent[j])
            self.handed.append(handed(x, self.distance))

        def place(self, j):
            edge = 0 if self.distance > 0 else chain - 1
            self.out = place(turns, self.handed[j], self.env, self.starts[j], self.out, scalars, edge)

    turns = Turns()
    left_op = jnp.transpose(left_mpo[0], (3, 1, 0, 2)).reshape(states * width, -1)
    right_op = jnp.transpose(right_mpo[0], (3, 0, 1, 2)).reshape(states * width, -1)
    left = Side(left_env, left_site, left_op, "i", "o", 2, 1)
    right = Side(right_env, right_site, right_op, "o", "i", 2 + inner * pair + outer, -1)
    both = (left, right)

    far = {}

    def gather(j):
        chunks = cut_columns(turns, [side.env for side in both], sum(cuts[:j]), cuts[j])
        for side, x in zip(both, chunks):
            side.own.append(x)
            far[side, j] = side.gather_far(x)

    def share(j, side):
        far[side, j] = side.share(turns.take(*far[side, j]))

    def first(side, j):
        side.first(j, far[side, j], 0, side.others * rows)

    for side in both:
        side.gather_near()
    gather(0)
    left.prepare(left.near + right.near)
    right.prepare([])
    gather(1)
    for side in both:
        side.prepare_bra([])
    share(0, left)
    share(0, right)
    first(left, 0)
    first(right, 0)
    share(1, left)
    left.begin()
    share(1, right)
    right.begin()
    first(left, 1)
    left.send(0)
    first(right, 1)
    right.send(0)
    left.send(1)
    right.send(1)
    left.keep(0)
    right.keep(0)
    right.send(2)
    right.keep(1)
    left.keep(1)
    left.place(0)
    right.place(0)
    right.keep(2)
    right.place(1)
    left.place(1)
    right.place(2)
    return (left.out[0][None], right.out[0][None])


def solution(mesh):
    return jax.shard_map(
        functools.partial(local, factors(mesh.shape["bond"])),
        mesh=mesh,
        in_specs=(
            P("site", "bond", None, None),
            P("site", "bond", None, None),
            P("site", None, None, None),
            P("site", None, None, None),
            P("site", None, None, None, None),
            P("site", None, None, None, None),
        ),
        out_specs=(P("site", "bond", None, None), P("site", "bond", None, None)),
        check_vma=False,
    )
```
